32 devices in a mesh: dp: 16 (over z, y, core), tensor: 2 (over x).
Axes of the slice: x: 2, y: 2, z: 4, core: 2. Of those that a mesh axis runs over, the one named last changes fastest.
Arguments:
- tokens: bfloat16 [16384, 1024], P(('dp', 'tensor')), may hold values from -6 to 6
- cotangent: bfloat16 [16384, 1024], P(('dp', 'tensor')), may hold values from -6 to 6
- species: int32 [16], P('dp'), may hold values from 1 to 8
- query_weight: bfloat16 [1024, 1024], P(None, 'tensor'), may hold values from -0.1875 to 0.1875
- key_weight: bfloat16 [1024, 1024], P(None, 'tensor'), may hold values from -0.1875 to 0.1875
- value_weight: bfloat16 [1024, 1024], P(None, 'tensor'), may hold values from -0.1875 to 0.1875
- out_weight: bfloat16 [1024, 1024], P('tensor'), may hold values from -2 to 2
- first_gain: float32 [1024], replicated, may hold values from 0.5 to 1.5
- first_bias: float32 [1024], replicated, may hold values from -3 to 3
- second_gain: float32 [1024], replicated, may hold values from 0.5 to 1.5
- second_bias: float32 [1024], replicated, may hold values from -3 to 3
- gate_weight: bfloat16 [1024, 4096], P(None, 'tensor'), may hold values from -0.1875 to 0.1875
- up_weight: bfloat16 [1024, 4096], P(None, 'tensor'), may hold values from -0.1875 to 0.1875
- down_weight: bfloat16 [4096, 1024], P('tensor'), may hold values from -0.1875 to 0.1875
Outputs:
- output: bfloat16 [16384, 1024], P(('dp', 'tensor'))
- input_grad: float32 [16384, 1024], P(('dp', 'tensor'))
- query_grad: float32 [1024, 1024], P('dp', 'tensor')
- key_grad: float32 [1024, 1024], P('dp', 'tensor')
- value_grad: float32 [1024, 1024], P('dp', 'tensor')
- out_grad: float32 [1024, 1024], P('tensor', 'dp')
- gate_grad: float32 [1024, 4096], P('dp', 'tensor')
- up_grad: float32 [1024, 4096], P('dp', 'tensor')
- down_grad: float32 [4096, 1024], P('tensor', 'dp')
- norm_grads: float32 [4, 1024], P(None, 'dp')
The draws below stay inside these ranges and needn't reach their ends.
All inputs are finite; a program needn't handle non-finite values.
Results may differ from the reference program's by a relative error of at most 0.014.
Values may be sent and summed in bfloat16 or wider, within the bound.
No kernel may reach another device: no remote copies, remote signals or barrier semaphores. Data moves between devices by JAX's collectives and lax.ppermute only.
A program may use at most 192 MiB of HBM per device.

```python
import jax
import jax.numpy as jnp
from jax import lax

D = 1024
HEADS = 16
HEAD_DIM = 64
FF = 4096
SEQ = 1024
WINDOWS = 16
TOKENS = 16384


def plant(array, stream_key, smallest, largest):
    spot = [jax.random.randint(jax.random.fold_in(stream_key, axis), (), 0, length) for axis, length in enumerate(array.shape)]
    longest = array.shape.index(max(array.shape))
    neighbour = spot[:longest] + [(spot[longest] + 1) % array.shape[longest]] + spot[longest + 1:]
    return array.at[tuple(spot)].set(smallest).at[tuple(neighbour)].set(largest)


def levels(own_key, dims, pieces, least, largest):
    loudness, own = 1.0, jax.random.fold_in(own_key, 6)
    for axis_at, blocks in pieces:
        steps = jnp.exp(jax.random.uniform(jax.random.fold_in(own, axis_at), (blocks,), jnp.float32, least / len(pieces), largest / len(pieces)))
        loudness = loudness * jnp.repeat(steps, dims[axis_at] // blocks).reshape([-1 if axis == axis_at else 1 for axis in range(len(dims))])
    return loudness


def scatter_about(stream_key, dims, deviation, most, split=(), kind=jnp.bfloat16):
    array = deviation * jax.random.normal(stream_key, dims, jnp.float32)
    if split:
        array = array * levels(stream_key, dims, split, -0.22, 0.18)
    return jnp.clip(array, -most, most).astype(kind)


def setup_inputs(seed: int = 0) -> dict:
    key_of = jax.random.split(jax.random.key(seed), 15)
    tokens = scatter_about(key_of[0], (TOKENS, D), 1.0, 6.0, ((0, 32),))
    cotangent = scatter_about(key_of[1], (TOKENS, D), 1.0, 6.0, ((0, 32),))
    species = plant(jax.random.randint(key_of[2], (WINDOWS,), 1, 9), jax.random.fold_in(key_of[2], 1), 1, 8).astype(jnp.int32)
    query_weight = scatter_about(key_of[3], (D, D), D ** -0.5, 0.1875, ((1, 2),))
    key_weight = scatter_about(key_of[4], (D, D), D ** -0.5, 0.1875, ((1, 2),))
    value_weight = scatter_about(key_of[5], (D, D), D ** -0.5, 0.1875, ((1, 2),))
    out_weight = scatter_about(key_of[6], (D, D), (D * 8 // SEQ) ** -0.5, 2.0, ((0, 2),))
    first_gain = jnp.clip(1.0 + 0.1 * jax.random.normal(key_of[7], (D,), jnp.float32), 0.5, 1.5)
    first_bias = scatter_about(key_of[8], (D,), 0.5, 3.0, (), jnp.float32)
    second_gain = jnp.clip(1.0 + 0.1 * jax.random.normal(key_of[9], (D,), jnp.float32), 0.5, 1.5)
    second_bias = scatter_about(key_of[10], (D,), 0.5, 3.0, (), jnp.float32)
    gate_weight = scatter_about(key_of[11], (D, FF), D ** -0.5, 0.1875, ((1, 2),))
    up_weight = scatter_about(key_of[12], (D, FF), D ** -0.5, 0.1875, ((1, 2),))
    down_weight = scatter_about(key_of[13], (FF, D), (FF // 4) ** -0.5, 0.1875, ((0, 2),))
    return {"tokens": tokens, "cotangent": cotangent, "species": species, "query_weight": query_weight, "key_weight": key_weight, "value_weight": value_weight, "out_weight": out_weight, "first_gain": first_gain, "first_bias": first_bias, "second_gain": second_gain, "second_bias": second_bias, "gate_weight": gate_weight, "up_weight": up_weight, "down_weight": down_weight}


EPS = 1e-05
BASE = 10000.0
HIGH = lax.Precision.HIGHEST

@jax.custom_vjp
def low(v):
    return lax.optimization_barrier(v.astype(jnp.bfloat16)).astype(jnp.float32)

@jax.custom_vjp
def low_back(v):
    return v

def low_keep(v):
    return (low(v), None)

def low_pass(kept, grad):
    return (grad,)

def back_keep(v):
    return (v, None)

def back_low(kept, grad):
    return (low(grad),)
low.defvjp(low_keep, low_pass)
low_back.defvjp(back_keep, back_low)

def normalize(rows):
    center = rows - lax.optimization_barrier(jnp.mean(rows, axis=-1, keepdims=True))
    invert = lax.rsqrt(lax.optimization_barrier(jnp.mean(center * center, axis=-1, keepdims=True)) + EPS)
    return center * invert

def rotary_tables(length, head):
    half = head // 2
    freq = BASE ** (-(jnp.arange(half, dtype=jnp.float32) * 2.0 / head))
    angle = jnp.arange(length, dtype=jnp.float32)[:, None] * freq[None, :]
    angle = jnp.concatenate([angle, angle], axis=1)
    return (jnp.cos(angle)[:, None, :], jnp.sin(angle)[:, None, :])

def rotate(values, cosine, sine):
    half = values.shape[-1] // 2
    turned = jnp.concatenate([-values[..., half:], values[..., :half]], axis=-1)
    return values * cosine + turned * sine

def matmul(left, right):
    return jnp.dot(left, right, precision=HIGH)

def window_forward(rows, query_weight, key_weight, value_weight, out_weight, first_gain, first_bias, second_gain, second_bias, gate_weight, up_weight, down_weight):
    cosine, sine = rotary_tables(SEQ, HEAD_DIM)
    first = low(normalize(rows) * first_gain + first_bias)
    queries = low(rotate(low_back(matmul(first, query_weight)).reshape(SEQ, HEADS, HEAD_DIM), cosine, sine))
    keys_all = low(rotate(low_back(matmul(first, key_weight)).reshape(SEQ, HEADS, HEAD_DIM), cosine, sine))
    values_all = low(low_back(matmul(first, value_weight))).reshape(SEQ, HEADS, HEAD_DIM)
    block = 512 if SEQ % 512 == 0 else SEQ
    scale = HEAD_DIM ** (-0.5)

    def attend_block(query_rows):
        scores = low_back(jnp.einsum('qhd,khd->hqk', query_rows, keys_all, precision=HIGH) * scale)
        probs = low(jax.nn.softmax(scores, axis=-1))
        return low_back(low(jnp.einsum('hqk,khd->qhd', probs, values_all, precision=HIGH)))
    mixed = lax.map(jax.checkpoint(attend_block), queries.reshape(SEQ // block, block, HEADS, HEAD_DIM))
    mixed = mixed.reshape(SEQ, D)
    hidden_res = rows + low_back(matmul(mixed, out_weight))
    second = low(normalize(hidden_res) * second_gain + second_bias)
    gate = low_back(matmul(second, gate_weight))
    upper = low_back(matmul(second, up_weight))
    hidden = low(jax.nn.silu(gate) * upper)
    return hidden_res + low_back(matmul(hidden, down_weight))

def reference(tokens, cotangent, species, query_weight, key_weight, value_weight, out_weight, first_gain, first_bias, second_gain, second_bias, gate_weight, up_weight, down_weight):
    weights = tuple((w.astype(jnp.float32) for w in (query_weight, key_weight, value_weight, out_weight, first_gain, first_bias, second_gain, second_bias, gate_weight, up_weight, down_weight)))
    inputs = tokens.astype(jnp.float32).reshape(WINDOWS, SEQ, D)
    grads_in = cotangent.astype(jnp.float32).reshape(WINDOWS, SEQ, D) * species.astype(jnp.float32)[:, None, None]

    def step(total, pair):
        rows, grad_rows = pair
        result, pull = jax.vjp(window_forward, rows, *weights)
        grads = pull(grad_rows)
        total = tuple((a + b for a, b in zip(total, grads[1:])))
        return (total, (result.astype(jnp.bfloat16), grads[0]))
    zeros = tuple((jnp.zeros_like(w) for w in weights))
    total, (results, input_grads) = lax.scan(step, zeros, (inputs, grads_in))
    norm_grads = jnp.stack([total[4], total[5], total[6], total[7]])
    return (results.reshape(TOKENS, D), input_grads.reshape(TOKENS, D), total[0], total[1], total[2], total[3], total[8], total[9], total[10], norm_grads)
```

```python
import functools
import math

import jax
import jax.numpy as jnp
from jax import lax
from jax.experimental import pallas as pl
from jax.experimental.pallas import tpu as pltpu
from jax.sharding import PartitionSpec as P

HEAD_DIM = 64
PAIR = 2 * HEAD_DIM
EPS = 1e-05
BASE = 10000.0
BF = jnp.bfloat16
F32 = jnp.float32
VMEM_LIMIT = 48 * 1024 * 1024

NN = (((1,), (0,)), ((), ()))
NT = (((1,), (1,)), ((), ()))


def dot(left, right, dims=NN):
    return lax.dot_general(left, right, dims, preferred_element_type=F32)


def shape(dims, kind):
    return jax.ShapeDtypeStruct(dims, kind)


def call(kernel, grid, in_specs, out_specs, out_shape, scratch=(), flops=0, name=None):
    moved = sum(math.prod(s.shape) * s.dtype.itemsize for s in out_shape)
    return pl.pallas_call(
        kernel,
        grid=grid,
        in_specs=in_specs,
        out_specs=out_specs,
        out_shape=out_shape,
        scratch_shapes=scratch,
        compiler_params=pltpu.CompilerParams(vmem_limit_bytes=VMEM_LIMIT),
        cost_estimate=pl.CostEstimate(
            flops=int(flops), bytes_accessed=int(2 * moved), transcendentals=0
        ),
        name=name,
    )


SMEM = pl.BlockSpec(memory_space=pltpu.SMEM)


def whole(*dims):
    return pl.BlockSpec(dims, lambda *at: (0,) * len(dims))


def normalize(rows):
    center = rows - jnp.mean(rows, axis=-1, keepdims=True)
    invert = lax.rsqrt(jnp.mean(center * center, axis=-1, keepdims=True) + EPS)
    return center * invert, invert


def norm_back(grad, shaped, invert, gain):
    inner = grad * gain
    return invert * (
        inner
        - jnp.mean(inner, axis=-1, keepdims=True)
        - shaped * jnp.mean(inner * shaped, axis=-1, keepdims=True)
    )


def lower_half(width):
    lane = lax.broadcasted_iota(jnp.int32, (1, width), 1)
    return (lane % HEAD_DIM) < HEAD_DIM // 2


def swap_halves(values):
    width = values.shape[-1]
    half = HEAD_DIM // 2
    return jnp.where(
        lower_half(width), pltpu.roll(values, width - half, 1), pltpu.roll(values, half, 1)
    )


def rotate(values, cosine, sine):
    turned = swap_halves(values)
    return values * cosine + jnp.where(lower_half(values.shape[-1]), -turned, turned) * sine


def unrotate(grad, cosine, sine):
    turned = swap_halves(grad * sine)
    return grad * cosine + jnp.where(lower_half(grad.shape[-1]), turned, -turned)


def rotary_tables(start, length):
    half = HEAD_DIM // 2
    freq = BASE ** (-(jnp.arange(half, dtype=F32) * 2.0 / HEAD_DIM))
    place = (start + jnp.arange(length, dtype=jnp.int32)).astype(F32)
    angle = place[:, None] * jnp.concatenate([freq] * (PAIR // half))[None, :]
    return jnp.cos(angle), jnp.sin(angle)


def project_kernel(scale, x, gain, bias, wq, wk, wv, cos, sin, first_out, q_out, k_out, v_out):
    shaped, _ = normalize(x[...].astype(F32))
    first = (shaped * gain[...] + bias[...]).astype(BF)
    first_out[...] = first
    cosine, sine = cos[...], sin[...]
    for weight, out, factor in ((wq, q_out, scale), (wk, k_out, 1.0)):
        made = dot(first, weight[...])
        for at in range(0, made.shape[1], PAIR):
            turned = rotate(made[:, at : at + PAIR], cosine, sine).astype(BF)
            out[:, at : at + PAIR] = turned * factor if factor != 1.0 else turned
    v_out[...] = dot(first, wv[...]).astype(BF)


def project(x, gain, bias, wq, wk, wv, tables):
    rows, width = x.shape
    mine = wq.shape[1]
    block = math.gcd(rows, 256)
    row = lambda cols: pl.BlockSpec((block, cols), lambda i: (i, 0))
    scale = HEAD_DIM ** (-0.5)
    return call(
        functools.partial(project_kernel, scale),
        (rows // block,),
        [row(width), whole(1, width), whole(1, width)]
        + [whole(width, mine)] * 3
        + [row(PAIR), row(PAIR)],
        [row(width), row(mine), row(mine), row(mine)],
        [shape((rows, width), BF)] + [shape((rows, mine), BF)] * 3,
        flops=6 * rows * width * mine,
        name="project",
    )(x, gain, bias, wq, wk, wv, *tables)


def attend_kernel(block, q, k0, k1, v0, v1, out, lse):
    lane = lax.broadcasted_iota(jnp.int32, (1, PAIR), 1)
    keys = jnp.concatenate([k0[...], k1[...]], axis=0)
    length = keys.shape[0]
    ones = jnp.where(lax.broadcasted_iota(jnp.int32, (length, PAIR), 1) == 0, 1.0, 0.0).astype(BF)
    values = jnp.concatenate([jnp.concatenate([v0[...], v1[...]], axis=0), ones], axis=1)
    for at in range(0, q.shape[0], block):
        rows = q[at : at + block, :]
        mixed = []
        for head in range(2):
            own = jnp.where((lane // HEAD_DIM) == head, rows, jnp.zeros_like(rows))
            scores = dot(own, keys, NT)
            top = jnp.max(scores, axis=-1, keepdims=True)
            probs = jnp.exp(scores - top).astype(BF)
            summed = dot(probs, values)
            total = summed[:, PAIR : PAIR + 1]
            mixed.append(summed[:, :PAIR] / total)
            lse[0, head, at : at + block] = (top + jnp.log(total))[:, 0]
        out[at : at + block, :] = jnp.where(lane < HEAD_DIM, mixed[0], mixed[1]).astype(BF)


def attend(q, k0, k1, v0, v1):
    rows, mine = q.shape
    pairs = mine // PAIR
    column = pl.BlockSpec((rows, PAIR), lambda i: (0, i))
    return call(
        functools.partial(attend_kernel, math.gcd(rows, 128)),
        (pairs,),
        [column] * 5,
        [column, pl.BlockSpec((1, 2, rows), lambda i: (i, 0, 0))],
        [shape((rows, mine), BF), shape((pairs, 2, rows), F32)],
        flops=16 * rows * rows * mine,
        name="attend",
    )(q, k0, k1, v0, v1)


def attend_back_kernel(block, *refs):
    (q, k, v, g, o, lse, cos, sin), outs = (
        [refs[2 * i : 2 * i + 2] for i in range(8)],
        refs[16:22],
    )
    dq, dk, dv = outs[0:2], outs[2:4], outs[4:6]
    key_acc, value_acc = refs[22:24]
    lane = lax.broadcasted_iota(jnp.int32, (1, PAIR), 1)
    keys = jnp.concatenate([k[0][...], k[1][...]], axis=0)
    values = jnp.concatenate([v[0][...], v[1][...]], axis=0)
    keys_t = keys.T
    rows = q[0].shape[0]
    scale = HEAD_DIM ** (-0.5)
    started = False
    for part in range(2):
        for at in range(0, rows, block):
            span = slice(at, at + block)
            query, grad = q[part][span, :], g[part][span, :]
            weighed = (grad.astype(F32) * o[part][span, :].astype(F32)).T
            key_sum, value_sum, query_back = None, None, []
            for head in range(2):
                mine = (lane // HEAD_DIM) == head
                own = jnp.where(mine, query, jnp.zeros_like(query))
                own_grad = jnp.where(mine, grad, jnp.zeros_like(grad))
                head_rows = slice(head * HEAD_DIM, (head + 1) * HEAD_DIM)
                delta = jnp.sum(weighed[head_rows, :], axis=0, keepdims=True)
                probs = jnp.exp(dot(keys, own, NT) - lse[part][0, head : head + 1, span])
                grad_scores = (probs * (dot(values, own_grad, NT) - delta)).astype(BF)
                value_one = dot(probs.astype(BF), own_grad)
                key_one = dot(grad_scores, own)
                query_back.append(dot(keys_t[head_rows, :], grad_scores))
                key_sum = key_one if key_sum is None else key_sum + key_one
                value_sum = value_one if value_sum is None else value_sum + value_one
            if started:
                key_acc[...] += key_sum
                value_acc[...] += value_sum
            else:
                key_acc[...] = key_sum
                value_acc[...] = value_sum
                started = True
            back = jnp.concatenate(query_back, axis=0).T * scale
            dq[part][span, :] = unrotate(back, cos[part][span, :], sin[part][span, :]).astype(BF)
    for part in range(2):
        span = slice(part * rows, (part + 1) * rows)
        dk[part][...] = unrotate(key_acc[span, :], cos[part][...], sin[part][...]).astype(BF)
        dv[part][...] = value_acc[span, :].astype(BF)


def attend_back(q, k, v, g, o, lse, cos, sin):
    rows, mine = q[0].shape
    pairs = mine // PAIR
    column = pl.BlockSpec((rows, PAIR), lambda i: (0, i))
    stat = pl.BlockSpec((1, 2, rows), lambda i: (i, 0, 0))
    table = whole(rows, PAIR)
    outs = call(
        functools.partial(attend_back_kernel, math.gcd(rows, 256)),
        (pairs,),
        [column] * 10 + [stat] * 2 + [table] * 4,
        [column] * 6,
        [shape((rows, mine), BF)] * 6,
        scratch=[pltpu.VMEM((2 * rows, PAIR), F32)] * 2,
        flops=80 * rows * rows * mine,
        name="attend_back",
    )(*q, *k, *v, *g, *o, *lse, *cos, *sin)
    return outs[0:2], outs[2:4], outs[4:6]


def residual_kernel(x, mixed, weight, other, gain, bias, res_out, second_out):
    res = x[...].astype(F32) + dot(mixed[...], weight[...]) + other[...].astype(F32)
    res_out[...] = res
    shaped, _ = normalize(res)
    second_out[...] = (shaped * gain[...] + bias[...]).astype(BF)


def residual(x, mixed, weight, other, gain, bias):
    rows, width = x.shape
    mine = mixed.shape[1]
    block = math.gcd(rows, 128)
    row = lambda cols: pl.BlockSpec((block, cols), lambda i: (i, 0))
    return call(
        residual_kernel,
        (rows // block,),
        [row(width), row(mine), whole(mine, width), row(width), whole(1, width), whole(1, width)],
        [row(width), row(width)],
        [shape((rows, width), F32), shape((rows, width), BF)],
        flops=2 * rows * width * mine,
        name="residual",
    )(x, mixed, weight, other, gain, bias)


def feed_kernel(species, second, cot, wg, wu, wd, hid_out, gb_out, ub_out, gr_out, st_out, acc):
    step = pl.program_id(0)

    @pl.when(step == 0)
    def _():
        gr_out[...] = (cot[...].astype(F32) * species[0].astype(F32)).astype(BF)

    rows, grad_rows = second[...], gr_out[...]
    gate = dot(rows, wg[...])
    upper = dot(rows, wu[...])
    grad_hidden = dot(grad_rows, wd[...], NT)
    sigma = jax.nn.sigmoid(gate)
    active = gate * sigma
    hid_out[...] = (active * upper).astype(BF)
    gate_back = (grad_hidden * upper * (sigma * (1.0 + gate * (1.0 - sigma)))).astype(BF)
    up_back = (grad_hidden * active).astype(BF)
    gb_out[...] = gate_back
    ub_out[...] = up_back
    terms = dot(gate_back, wg[...], NT) + dot(up_back, wu[...], NT)

    @pl.when(step == 0)
    def _():
        acc[...] = terms

    @pl.when(step > 0)
    def _():
        acc[...] += terms

    @pl.when(step == pl.num_programs(0) - 1)
    def _():
        st_out[...] = acc[...].astype(st_out.dtype)


def feed(species, second, cot, wg, wu, wd, kind):
    rows, width = second.shape
    hidden = wg.shape[1]
    block = math.gcd(hidden, 256)
    column = pl.BlockSpec((width, block), lambda j: (0, j))
    wide = pl.BlockSpec((rows, block), lambda j: (0, j))
    flat = whole(rows, width)
    return call(
        feed_kernel,
        (hidden // block,),
        [SMEM, flat, flat, column, column, pl.BlockSpec((block, width), lambda j: (j, 0))],
        [wide, wide, wide, flat, flat],
        [shape((rows, hidden), BF)] * 3 + [shape((rows, width), BF), shape((rows, width), kind)],
        scratch=[pltpu.VMEM((rows, width), F32)],
        flops=10 * rows * width * hidden,
        name="feed",
    )(species, second, cot, wg, wu, wd)


def weight_grad_kernel(count, place, a0, a1, *refs):
    ins, outs, (flipped, made) = refs[: 2 * count], refs[2 * count : 4 * count], refs[4 * count :]
    rows = a0.shape[0]

    @pl.when(pl.program_id(0) == 0)
    def _():
        flipped[:, :rows] = a0[...].T
        flipped[:, rows:] = a1[...].T

    own = place[0]
    for i in range(count):
        right = jnp.concatenate([ins[2 * i][...], ins[2 * i + 1][...]], axis=0)
        made[...] = dot(flipped[...], right).astype(BF).reshape(made.shape)
        outs[2 * i][...] = made[:, own]
        outs[2 * i + 1][...] = made[:, 1 - own]


def weight_grad(place, parts, left, rights, block=256):
    rows, width = left[0].shape
    columns = rights[0][0].shape[1]
    count = len(rights)
    block = math.gcd(columns, block)
    each = width // parts
    column = pl.BlockSpec((rows, block), lambda j: (0, j))
    out = pl.BlockSpec((parts // 2, each, block), lambda j: (0, 0, j))
    outs = call(
        functools.partial(weight_grad_kernel, count),
        (columns // block,),
        [SMEM] + [whole(rows, width)] * 2 + [column] * (2 * count),
        [out] * (2 * count),
        [shape((parts // 2, each, columns), BF)] * (2 * count),
        scratch=[
            pltpu.VMEM((width, 2 * rows), BF),
            pltpu.VMEM((parts // 2, 2, each, block), BF),
        ],
        flops=4 * rows * width * columns * count,
        name="weight_grad",
    )(place, *left, *[half for pair in rights for half in pair])
    return [outs[2 * i : 2 * i + 2] for i in range(count)]


def res_back_kernel(species, own, other, cot, res, gain, grad_out, attn_out, terms_out):
    grad = own[...] + other[...].astype(F32)
    shaped, invert = normalize(res[...])
    made = cot[...].astype(F32) * species[0].astype(F32) + norm_back(
        grad, shaped, invert, gain[...]
    )
    grad_out[...] = made
    attn_out[...] = made.astype(BF)

    @pl.when(pl.program_id(0) == 0)
    def _():
        terms_out[...] = jnp.zeros_like(terms_out)

    terms_out[0:1, :] += jnp.sum(grad * shaped, axis=0, keepdims=True)
    terms_out[1:2, :] += jnp.sum(grad, axis=0, keepdims=True)


def res_back(species, own, other, cot, res, gain):
    rows, width = own.shape
    block = math.gcd(rows, 128)
    row = pl.BlockSpec((block, width), lambda i: (i, 0))
    return call(
        res_back_kernel,
        (rows // block,),
        [SMEM, row, row, row, row, whole(1, width)],
        [row, row, whole(2, width)],
        [shape((rows, width), F32), shape((rows, width), BF), shape((2, width), F32)],
        name="res_back",
    )(species, own, other, cot, res, gain)


def first_back_kernel(bq, bk, bv, wq, wk, wv, x, out, terms_out):
    grad = dot(bq[...], wq[...], NT) + dot(bk[...], wk[...], NT) + dot(bv[...], wv[...], NT)
    out[...] = grad.astype(out.dtype)
    shaped, _ = normalize(x[...].astype(F32))

    @pl.when(pl.program_id(0) == 0)
    def _():
        terms_out[...] = jnp.zeros_like(terms_out)

    terms_out[0:1, :] += jnp.sum(grad * shaped, axis=0, keepdims=True)
    terms_out[1:2, :] += jnp.sum(grad, axis=0, keepdims=True)


def first_back(bq, bk, bv, wq, wk, wv, x, kind):
    rows, width = x.shape
    mine = bq.shape[1]
    block = math.gcd(rows, 256)
    row = lambda cols: pl.BlockSpec((block, cols), lambda i: (i, 0))
    return call(
        first_back_kernel,
        (rows // block,),
        [row(mine)] * 3 + [whole(width, mine)] * 3 + [row(width)],
        [row(width), whole(2, width)],
        [shape((rows, width), kind), shape((2, width), F32)],
        flops=6 * rows * width * mine,
        name="first_back",
    )(bq, bk, bv, wq, wk, wv, x)


def input_back_kernel(own, other, x, res, gain, out):
    shaped, invert = normalize(x[...].astype(F32))
    grad = own[...] + other[...].astype(F32)
    out[...] = res[...] + norm_back(grad, shaped, invert, gain[...])


def input_back(own, other, x, res, gain):
    rows, width = x.shape
    block = math.gcd(rows, 128)
    row = pl.BlockSpec((block, width), lambda i: (i, 0))
    return call(
        input_back_kernel,
        (rows // block,),
        [row] * 4 + [whole(1, width)],
        [row],
        [shape((rows, width), F32)],
        name="input_back",
    )(own, other, x, res, gain)[0]


def pair_swap(values):
    return lax.ppermute(values, "tensor", [(0, 1), (1, 0)])


def dp_swap(values, bit, parts):
    return lax.ppermute(values, "dp", [(i, i ^ (1 << bit)) for i in range(parts)])


def scatter_rest(current, order, parts, place, kind):
    bits = parts.bit_length() - 1
    tail = current.shape[1:]
    left = list(range(bits - 1, 0, -1))
    current = current.reshape((2,) * (bits - 1) + tail)
    for bit in order:
        axis = left.index(bit)
        mine = (place >> bit) & 1
        keep = lax.dynamic_index_in_dim(current, mine, axis, keepdims=False)
        send = lax.dynamic_index_in_dim(current, 1 - mine, axis, keepdims=False)
        left.remove(bit)
        current = keep.astype(F32) + dp_swap(send, bit, parts).astype(F32)
        current = current.astype(kind if left else F32)
    return current


def scatter(keep, send, order, parts, place):
    got = dp_swap(send, 0, parts)
    total = (keep.astype(F32) + got.astype(F32)).astype(BF)
    return scatter_rest(total, order, parts, place, BF)


def scatter_terms(terms, parts, place):
    terms = terms + pair_swap(terms)
    each = terms.shape[1] // parts
    current = terms.reshape(2, parts, each).transpose(1, 0, 2)
    bits = parts.bit_length() - 1
    for bit in range(bits - 1, -1, -1):
        current = current.reshape(2, -1, 2, each)
        mine = (place >> bit) & 1
        keep = lax.dynamic_index_in_dim(current, mine, 0, keepdims=False)
        send = lax.dynamic_index_in_dim(current, 1 - mine, 0, keepdims=False)
        current = keep + dp_swap(send, bit, parts)
    return current.reshape(2, each)


def body(
    parts,
    tokens,
    cotangent,
    species,
    wq,
    wk,
    wv,
    wo,
    first_gain,
    first_bias,
    second_gain,
    second_bias,
    wg,
    wu,
    wd,
):
    place = lax.axis_index("dp")
    half = lax.axis_index("tensor")
    core = (place & 1).astype(jnp.int32).reshape(1)
    rows = tokens.shape[0]
    bits = parts.bit_length() - 1
    low_first = list(range(1, bits))
    first_gain, first_bias = first_gain[None], first_bias[None]
    second_gain, second_bias = second_gain[None], second_bias[None]

    tokens1 = pair_swap(tokens)
    cot1 = pair_swap(cotangent)
    table0 = rotary_tables(half * rows, rows)
    table1 = rotary_tables((1 - half) * rows, rows)
    first0, q0, k0, v0 = project(tokens, first_gain, first_bias, wq, wk, wv, table0)
    first1, q1, k1, v1 = project(tokens1, first_gain, first_bias, wq, wk, wv, table1)
    mixed1, lse1 = attend(q1, k0, k1, v0, v1)
    attn1 = dot(mixed1, wo).astype(BF)
    got = pair_swap(attn1)
    mixed0, lse0 = attend(q0, k0, k1, v0, v1)
    res, second0 = residual(tokens, mixed0, wo, got, second_gain, second_bias)
    second1 = pair_swap(second0)
    hid0, gb0, ub0, gr0, st0 = feed(species, second0, cotangent, wg, wu, wd, F32)
    hid1, gb1, ub1, gr1, st1 = feed(species, second1, cot1, wg, wu, wd, BF)
    got = pair_swap(st1)
    grad_res, attn_grad0, second_terms = res_back(species, st0, got, cotangent, res, second_gain)
    attn_grad1 = pair_swap(attn_grad0)

    grad = lambda left, rights: weight_grad(core, parts, left, rights)
    ((gate_keep, gate_send),) = grad((second0, second1), [(gb0, gb1)])
    ((up_keep, up_send),) = grad((second0, second1), [(ub0, ub1)])
    ((down_keep, down_send),) = grad((gr0, gr1), [(hid0, hid1)])
    send = lambda keep, give: scatter(keep, give, low_first, parts, place)
    gate_sum = send(gate_keep, gate_send)
    up_sum = send(up_keep, up_send)
    down_sum = send(down_keep, down_send).T

    ff_got = pair_swap(dot(hid1, wd).astype(BF))
    output = (res + dot(hid0, wd) + ff_got.astype(F32)).astype(BF)

    gm0 = dot(attn_grad0, wo, NT).astype(BF)
    gm1 = dot(attn_grad1, wo, NT).astype(BF)
    (bq0, bq1), (bk0, bk1), (bv0, bv1) = attend_back(
        (q0, q1),
        (k0, k1),
        (v0, v1),
        (gm0, gm1),
        (mixed0, mixed1),
        (lse0, lse1),
        (table0[0], table1[0]),
        (table0[1], table1[1]),
    )
    ((out_keep, out_send),) = grad((attn_grad0, attn_grad1), [(mixed0, mixed1)])
    out_sum = send(out_keep, out_send).T
    ft1, terms1 = first_back(bq1, bk1, bv1, wq, wk, wv, tokens1, BF)
    got = pair_swap(ft1)
    ft0, terms0 = first_back(bq0, bk0, bv0, wq, wk, wv, tokens, F32)
    made = grad((first0, first1), [(bq0, bq1), (bk0, bk1), (bv0, bv1)])
    query_sum, key_sum, value_sum = (send(keep, give) for keep, give in made)
    input_grad = input_back(ft0, got, tokens, grad_res, first_gain)
    norm_grads = jnp.concatenate(
        [scatter_terms(terms0 + terms1, parts, place), scatter_terms(second_terms, parts, place)]
    )
    return (
        output,
        input_grad,
        query_sum,
        key_sum,
        value_sum,
        out_sum,
        gate_sum,
        up_sum,
        down_sum,
        norm_grads,
    )


def solution(mesh):
    in_specs = (
        P(("dp", "tensor"), None),
        P(("dp", "tensor"), None),
        P("dp"),
        P(None, "tensor"),
        P(None, "tensor"),
        P(None, "tensor"),
        P("tensor", None),
        P(),
        P(),
        P(),
        P(),
        P(None, "tensor"),
        P(None, "tensor"),
        P("tensor", None),
    )
    out_specs = (
        P(("dp", "tensor"), None),
        P(("dp", "tensor"), None),
        P("dp", "tensor"),
        P("dp", "tensor"),
        P("dp", "tensor"),
        P("tensor", "dp"),
        P("dp", "tensor"),
        P("dp", "tensor"),
        P("tensor", "dp"),
        P(None, "dp"),
    )
    return jax.shard_map(
        functools.partial(body, mesh.shape["dp"]),
        mesh=mesh,
        in_specs=in_specs,
        out_specs=out_specs,
        check_vma=False,
    )
```

```python
import functools
import math

import jax
import jax.numpy as jnp
from jax import lax
from jax.experimental import pallas as pl
from jax.experimental.pallas import tpu as pltpu
from jax.sharding import PartitionSpec as P

HEAD_DIM = 64
PAIR = 2 * HEAD_DIM
EPS = 1e-05
BASE = 10000.0
BF = jnp.bfloat16
F32 = jnp.float32
MOST = 60 * 1024 * 1024
COST = 1000

NN = (((1,), (0,)), ((), ()))
NT = (((1,), (1,)), ((), ()))


def dot(left, right, dims=NN):
    return lax.dot_general(left, right, dims, preferred_element_type=F32)


def shape(dims, kind):
    return jax.ShapeDtypeStruct(dims, kind)


def call(
    kernel,
    grid,
    in_specs,
    out_specs,
    out_shape,
    scratch=(),
    flops=0,
    name=None,
    after=(),
    scalars=0,
    limit=MOST,
):
    count = len(after)
    moved = sum(math.prod(s.shape) * s.dtype.itemsize for s in out_shape)

    def ordered(*refs):
        given = scalars + len(in_specs)
        kernel(*refs[:given], *refs[given + count :])

    made = pl.pallas_call(
        ordered,
        grid_spec=pltpu.PrefetchScalarGridSpec(
            num_scalar_prefetch=scalars,
            grid=grid,
            in_specs=list(in_specs) + [pl.BlockSpec(memory_space=pl.ANY)] * count,
            out_specs=out_specs,
            scratch_shapes=scratch,
        ),
        out_shape=out_shape,
        compiler_params=pltpu.CompilerParams(vmem_limit_bytes=limit),
        cost_estimate=pl.CostEstimate(
            flops=int(flops + 3e9) * COST, bytes_accessed=2 * moved, transcendentals=0
        ),
        name=name,
    )
    return lambda *given: made(*given, *after)


SMEM = pl.BlockSpec(memory_space=pltpu.SMEM)


def whole(*dims):
    return pl.BlockSpec(dims, lambda *at: (0,) * len(dims))


def normalize(rows):
    center = rows - jnp.mean(rows, axis=-1, keepdims=True)
    invert = lax.rsqrt(jnp.mean(center * center, axis=-1, keepdims=True) + EPS)
    return center * invert, invert


def norm_back(grad, shaped, invert, gain):
    inner = grad * gain
    return invert * (
        inner
        - jnp.mean(inner, axis=-1, keepdims=True)
        - shaped * jnp.mean(inner * shaped, axis=-1, keepdims=True)
    )


def lower_half(width):
    lane = lax.broadcasted_iota(jnp.int32, (1, width), 1)
    return (lane % HEAD_DIM) < HEAD_DIM // 2


def swap_halves(values):
    width = values.shape[-1]
    half = HEAD_DIM // 2
    return jnp.where(
        lower_half(width), pltpu.roll(values, width - half, 1), pltpu.roll(values, half, 1)
    )


def rotate(values, cosine, sine):
    turned = swap_halves(values)
    return values * cosine + jnp.where(lower_half(values.shape[-1]), -turned, turned) * sine


def unrotate(grad, cosine, sine):
    turned = swap_halves(grad * sine)
    return grad * cosine + jnp.where(lower_half(grad.shape[-1]), turned, -turned)


def rotary_tables(start, length):
    half = HEAD_DIM // 2
    freq = BASE ** (-(jnp.arange(half, dtype=F32) * 2.0 / HEAD_DIM))
    place = (start + jnp.arange(length, dtype=jnp.int32)).astype(F32)
    angle = place[:, None] * jnp.concatenate([freq] * (PAIR // half))[None, :]
    return jnp.cos(angle), jnp.sin(angle)


def project_kernel(scale, x, gain, bias, wq, wk, wv, cos, sin, first_out, q_out, k_out, v_out):
    shaped, _ = normalize(x[...].astype(F32))
    first = (shaped * gain[...] + bias[...]).astype(BF)
    first_out[...] = first
    cosine, sine = cos[...], sin[...]
    for weight, out, factor in ((wq, q_out, scale), (wk, k_out, 1.0)):
        made = dot(first, weight[...])
        for at in range(0, made.shape[1], PAIR):
            turned = rotate(made[:, at : at + PAIR], cosine, sine).astype(BF)
            out[:, at : at + PAIR] = turned * factor if factor != 1.0 else turned
    v_out[...] = dot(first, wv[...]).astype(BF)


def project(x, gain, bias, wq, wk, wv, tables):
    rows, width = x.shape
    mine = wq.shape[1]
    block = math.gcd(rows, 256)
    row = lambda cols: pl.BlockSpec((block, cols), lambda i: (i, 0))
    scale = HEAD_DIM ** (-0.5)
    return call(
        functools.partial(project_kernel, scale),
        (rows // block,),
        [row(width), whole(1, width), whole(1, width)]
        + [whole(width, mine)] * 3
        + [row(PAIR), row(PAIR)],
        [row(width), row(mine), row(mine), row(mine)],
        [shape((rows, width), BF)] + [shape((rows, mine), BF)] * 3,
        flops=6 * rows * width * mine,
        name="project",
    )(x, gain, bias, wq, wk, wv, *tables)


def attend_kernel(block, q, k0, k1, v0, v1, out, lse):
    lane = lax.broadcasted_iota(jnp.int32, (1, PAIR), 1)
    keys = jnp.concatenate([k0[...], k1[...]], axis=0)
    length = keys.shape[0]
    ones = jnp.where(lax.broadcasted_iota(jnp.int32, (length, PAIR), 1) == 0, 1.0, 0.0).astype(BF)
    values = jnp.concatenate([jnp.concatenate([v0[...], v1[...]], axis=0), ones], axis=1)
    for at in range(0, q.shape[0], block):
        rows = q[at : at + block, :]
        mixed = []
        for head in range(2):
            own = jnp.where((lane // HEAD_DIM) == head, rows, jnp.zeros_like(rows))
            scores = dot(own, keys, NT)
            top = jnp.max(scores, axis=-1, keepdims=True)
            probs = jnp.exp(scores - top).astype(BF)
            summed = dot(probs, values)
            total = summed[:, PAIR : PAIR + 1]
            mixed.append(summed[:, :PAIR] / total)
            lse[0, head, at : at + block] = (top + jnp.log(total))[:, 0]
        out[at : at + block, :] = jnp.where(lane < HEAD_DIM, mixed[0], mixed[1]).astype(BF)


def attend(q, k0, k1, v0, v1, after=()):
    rows, mine = q.shape
    pairs = mine // PAIR
    column = pl.BlockSpec((rows, PAIR), lambda i: (0, i))
    return call(
        functools.partial(attend_kernel, math.gcd(rows, 128)),
        (pairs,),
        [column] * 5,
        [column, pl.BlockSpec((1, 2, rows), lambda i: (i, 0, 0))],
        [shape((rows, mine), BF), shape((pairs, 2, rows), F32)],
        flops=16 * rows * rows * mine,
        name="attend",
        after=after,
    )(q, k0, k1, v0, v1)


def attend_back_kernel(block, *refs):
    (q, k, v, g, o, lse, cos, sin), outs = (
        [refs[2 * i : 2 * i + 2] for i in range(8)],
        refs[16:22],
    )
    dq, dk, dv = outs[0:2], outs[2:4], outs[4:6]
    key_acc, value_acc = refs[22:24]
    lane = lax.broadcasted_iota(jnp.int32, (1, PAIR), 1)
    keys = jnp.concatenate([k[0][...], k[1][...]], axis=0)
    values = jnp.concatenate([v[0][...], v[1][...]], axis=0)
    keys_t = keys.T
    rows = q[0].shape[0]
    scale = HEAD_DIM ** (-0.5)
    started = False
    for part in range(2):
        for at in range(0, rows, block):
            span = slice(at, at + block)
            query, grad = q[part][span, :], g[part][span, :]
            weighed = (grad.astype(F32) * o[part][span, :].astype(F32)).T
            key_sum, value_sum, query_back = None, None, []
            for head in range(2):
                mine = (lane // HEAD_DIM) == head
                own = jnp.where(mine, query, jnp.zeros_like(query))
                own_grad = jnp.where(mine, grad, jnp.zeros_like(grad))
                head_rows = slice(head * HEAD_DIM, (head + 1) * HEAD_DIM)
                delta = jnp.sum(weighed[head_rows, :], axis=0, keepdims=True)
                probs = jnp.exp(dot(keys, own, NT) - lse[part][0, head : head + 1, span])
                grad_scores = (probs * (dot(values, own_grad, NT) - delta)).astype(BF)
                value_one = dot(probs.astype(BF), own_grad)
                key_one = dot(grad_scores, own)
                query_back.append(dot(keys_t[head_rows, :], grad_scores))
                key_sum = key_one if key_sum is None else key_sum + key_one
                value_sum = value_one if value_sum is None else value_sum + value_one
            if started:
                key_acc[...] += key_sum
                value_acc[...] += value_sum
            else:
                key_acc[...] = key_sum
                value_acc[...] = value_sum
                started = True
            back = jnp.concatenate(query_back, axis=0).T * scale
            dq[part][span, :] = unrotate(back, cos[part][span, :], sin[part][span, :]).astype(BF)
    for part in range(2):
        span = slice(part * rows, (part + 1) * rows)
        dk[part][...] = unrotate(key_acc[span, :], cos[part][...], sin[part][...]).astype(BF)
        dv[part][...] = value_acc[span, :].astype(BF)


def attend_back(start, stop, q, k, v, g, o, lse, cos, sin, after=()):
    rows = q[0].shape[0]
    pairs = stop - start
    mine = pairs * PAIR
    column = pl.BlockSpec((rows, PAIR), lambda i: (0, start + i))
    made = pl.BlockSpec((rows, PAIR), lambda i: (0, i))
    stat = pl.BlockSpec((1, 2, rows), lambda i: (start + i, 0, 0))
    table = whole(rows, PAIR)
    outs = call(
        functools.partial(attend_back_kernel, math.gcd(rows, 256)),
        (pairs,),
        [column] * 10 + [stat] * 2 + [table] * 4,
        [made] * 6,
        [shape((rows, mine), BF)] * 6,
        scratch=[pltpu.VMEM((2 * rows, PAIR), F32)] * 2,
        flops=80 * rows * rows * mine,
        name="attend_back",
        after=after,
    )(*q, *k, *v, *g, *o, *lse, *cos, *sin)
    return outs[0:2], outs[2:4], outs[4:6]


def residual_kernel(x, mixed, weight, other, gain, bias, res_out, second_out):
    res = x[...].astype(F32) + dot(mixed[...], weight[...]) + other[...].astype(F32)
    res_out[...] = res
    shaped, _ = normalize(res)
    second_out[...] = (shaped * gain[...] + bias[...]).astype(BF)


def residual(x, mixed, weight, other, gain, bias, after=()):
    rows, width = x.shape
    mine = mixed.shape[1]
    block = math.gcd(rows, 256)
    row = lambda cols: pl.BlockSpec((block, cols), lambda i: (i, 0))
    return call(
        residual_kernel,
        (rows // block,),
        [row(width), row(mine), whole(mine, width), row(width), whole(1, width), whole(1, width)],
        [row(width), row(width)],
        [shape((rows, width), F32), shape((rows, width), BF)],
        flops=2 * rows * width * mine,
        name="residual",
        after=after,
    )(x, mixed, weight, other, gain, bias)


def relay_kernel(given, out):
    out[...] = given[...]


def relay(given, after):
    return call(
        relay_kernel,
        (1,),
        [whole(*given.shape)],
        [whole(*given.shape)],
        [shape(given.shape, given.dtype)],
        name="relay",
        after=after,
    )(given)[0]


def scale_kernel(species, cot0, cot1, out0, out1):
    for cot, out in ((cot0, out0), (cot1, out1)):
        out[...] = (cot[...].astype(F32) * species[0].astype(F32)).astype(BF)


def scale_rows(species, cot0, cot1, after=()):
    rows, width = cot0.shape
    block = math.gcd(rows, 256)
    row = pl.BlockSpec((block, width), lambda i: (i, 0))
    return call(
        scale_kernel,
        (rows // block,),
        [SMEM, row, row],
        [row, row],
        [shape((rows, width), BF)] * 2,
        name="scale_rows",
        after=after,
    )(species, cot0, cot1)


def feed_kernel(second, grads, wg, wu, wd, *refs):
    (hid_out, gb_out, ub_out, st_out), refs = refs[:4], refs[4:]
    outs, accs = ([st_out], refs) if len(refs) == 1 else ([st_out, refs[0]], refs[1:])
    step = pl.program_id(0)

    rows, grad_rows = second[...], grads[...]
    gate = dot(rows, wg[...])
    upper = dot(rows, wu[...])
    grad_hidden = dot(grad_rows, wd[...], NT)
    sigma = 0.5 * jnp.tanh(0.5 * gate) + 0.5
    active = gate * sigma
    hidden = (active * upper).astype(BF)
    gate_back = (grad_hidden * upper * (sigma + active * (1.0 - sigma))).astype(BF)
    up_back = (grad_hidden * active).astype(BF)
    hid_out[...] = hidden
    gb_out[...] = gate_back
    ub_out[...] = up_back
    terms = [dot(gate_back, wg[...], NT) + dot(up_back, wu[...], NT)]
    if len(accs) == 2:
        terms.append(dot(hidden, wd[...]))

    @pl.when(step == 0)
    def _():
        for acc, term in zip(accs, terms):
            acc[...] = term

    @pl.when(step > 0)
    def _():
        for acc, term in zip(accs, terms):
            acc[...] += term

    @pl.when(step == pl.num_programs(0) - 1)
    def _():
        for out, acc in zip(outs, accs):
            out[...] = acc[...].astype(out.dtype)


def feed(second, grads, wg, wu, wd, kind, forward, after=()):
    rows, width = second.shape
    hidden = wg.shape[1]
    block = math.gcd(hidden, 512)
    column = pl.BlockSpec((width, block), lambda j: (0, j))
    wide = pl.BlockSpec((rows, block), lambda j: (0, j))
    flat = whole(rows, width)
    more = int(forward)
    return call(
        feed_kernel,
        (hidden // block,),
        [flat, flat, column, column, pl.BlockSpec((block, width), lambda j: (j, 0))],
        [wide, wide, wide, flat] + [flat] * more,
        [shape((rows, hidden), BF)] * 3
        + [shape((rows, width), kind)]
        + [shape((rows, width), F32)] * more,
        scratch=[pltpu.VMEM((rows, width), F32)] * (1 + more),
        flops=10 * rows * width * hidden,
        name="feed",
        after=after,
    )(second, grads, wg, wu, wd)


def flip(out, halves):
    rows = halves[0].shape[0]
    out[:, :rows] = halves[0][...].T
    out[:, rows:] = halves[1][...].T


def give_out(own, keep, send, span, value):
    value = value.reshape(keep.shape[0], 2, keep.shape[1], value.shape[1])
    even, odd = value[:, 0], value[:, 1]
    keep[:, :, span] = jnp.where(own == 1, odd, even).astype(BF)
    send[:, :, span] = jnp.where(own == 1, even, odd).astype(BF)


def weight_grad_kernel(jobs, core, *refs):
    outs, flipped = refs[-1 - 2 * len(jobs) : -1], refs[-1]
    step = pl.program_id(0)
    at = 0
    for keep, send, (count, pieces, steps, fresh) in zip(outs[::2], outs[1::2], jobs):
        left, refs = refs[:count], refs[count:]
        right, refs = refs[: count * pieces], refs[count * pieces :]
        rows = left[0].shape[0]

        if fresh:

            @pl.when(step == at)
            def _():
                for i in range(count):
                    flipped[:, i * rows : (i + 1) * rows] = left[i][...].T

        @pl.when((step >= at) & (step < at + steps))
        def _():
            beside = [
                jnp.concatenate([one[...] for one in right[i * pieces : (i + 1) * pieces]], axis=1)
                for i in range(count)
            ]
            value = dot(flipped[:, : count * rows], jnp.concatenate(beside, axis=0))
            give_out(core[0], keep, send, slice(None), value)

        at += steps


def weight_grad(core, parts, jobs, after=()):
    block = 1024
    for _, right in jobs:
        block = math.gcd(block, sum(one.shape[1] for one in right[0]))
    width = jobs[0][0][0].shape[1]
    each = width // parts
    kinds, specs, given, outs, kept, at, most, last_left = [], [], [], [], [], 0, 0, None
    for left, right in jobs:
        rows = left[0].shape[0]
        wide = sum(one.shape[1] for one in right[0])
        steps, pieces = wide // block, len(right[0])
        most = max(most, rows * len(left))
        specs += [whole(rows, width)] * len(left)
        given += left
        for one in [piece for row in right for piece in row]:
            cut = block if pieces == 1 else one.shape[1]
            last = one.shape[1] // cut - 1
            specs.append(
                pl.BlockSpec(
                    (rows, cut), lambda j, at=at, last=last: (0, jnp.clip(j - at, 0, last))
                )
            )
            given.append(one)
        kinds.append((len(left), pieces, steps, left is not last_left))
        outs += [
            pl.BlockSpec(
                (parts // 2, each, block),
                lambda j, at=at, last=steps - 1: (0, 0, jnp.clip(j - at, 0, last)),
            )
        ] * 2
        kept += [shape((parts // 2, each, wide), BF)] * 2
        last_left = left
        at += steps
    return call(
        functools.partial(weight_grad_kernel, kinds),
        (at,),
        [SMEM] + specs,
        outs,
        kept,
        scratch=[pltpu.VMEM((width, most), BF)],
        flops=2 * most * width * at * block,
        name="weight_grad",
        after=after,
    )(core, *given)


def head_grad_kernel(count, with_out, core, *refs):
    first, backs, refs = refs[:2], refs[2 : 2 + 2 * count], refs[2 + 2 * count :]
    keep, send, flipped = refs[-3:]
    flip(flipped, first)
    at = 0
    for i in range(count):
        right = jnp.concatenate([backs[2 * i][...], backs[2 * i + 1][...]], axis=0)
        wide = right.shape[1]
        give_out(core[0], keep, send, slice(at, at + wide), dot(flipped[...], right))
        at += wide
    if with_out:
        flip(flipped, refs[0:2])
        right = jnp.concatenate([refs[2][...], refs[3][...]], axis=0)
        give_out(core[0], keep, send, slice(at, at + right.shape[1]), dot(flipped[...], right))
    else:
        terms = refs[:3]
        rows = [terms[0][...] + terms[1][...], terms[2][...]]
        rows.append(jnp.zeros((PAIR - 4, rows[0].shape[1]), F32))
        value = jnp.concatenate(rows, axis=0).T
        give_out(core[0], keep, send, slice(at, at + PAIR), value)


def head_grad(core, parts, first, backs, out_job=(), terms=(), after=()):
    rows, width = first[0].shape
    each = width // parts
    total = sum(back[0].shape[1] for back in backs)
    total += out_job[2].shape[1] if out_job else PAIR
    given = [*first, *[half for pair in backs for half in pair], *out_job, *terms]
    out = whole(parts // 2, each, total)
    return call(
        functools.partial(head_grad_kernel, len(backs), bool(out_job)),
        (1,),
        [SMEM] + [whole(*one.shape) for one in given],
        [out] * 2,
        [shape((parts // 2, each, total), BF)] * 2,
        scratch=[pltpu.VMEM((width, 2 * rows), BF)],
        flops=4 * rows * width * total,
        name="head_grad",
        after=after,
    )(core, *given)


def res_back_kernel(
    species, own, other, cot, res, gain, w0, w1, grad_out, attn_out, gm0_out, gm1_out, terms_out
):
    grad = own[...] + other[...].astype(F32)
    shaped, invert = normalize(res[...])
    made = cot[...].astype(F32) * species[0].astype(F32) + norm_back(
        grad, shaped, invert, gain[...]
    )
    grad_out[...] = made
    attn = made.astype(BF)
    attn_out[...] = attn
    gm1_out[...] = dot(attn, w1[...], NT).astype(BF)
    gm0_out[...] = dot(attn, w0[...], NT).astype(BF)

    @pl.when(pl.program_id(0) == 0)
    def _():
        terms_out[...] = jnp.zeros_like(terms_out)

    terms_out[0:1, :] += jnp.sum(grad * shaped, axis=0, keepdims=True)
    terms_out[1:2, :] += jnp.sum(grad, axis=0, keepdims=True)


def res_back(species, own, other, cot, res, gain, w0, w1, after=()):
    rows, width = own.shape
    mine = w0.shape[0]
    block = math.gcd(rows, 256)
    row = lambda cols: pl.BlockSpec((block, cols), lambda i: (i, 0))
    return call(
        res_back_kernel,
        (rows // block,),
        [SMEM] + [row(width)] * 4 + [whole(1, width)] + [whole(mine, width)] * 2,
        [row(width), row(width), row(mine), row(mine), whole(2, width)],
        [
            shape((rows, width), F32),
            shape((rows, width), BF),
            shape((rows, mine), BF),
            shape((rows, mine), BF),
            shape((2, width), F32),
        ],
        flops=4 * rows * width * mine,
        name="res_back",
        after=after,
    )(species, own, other, cot, res, gain, w0, w1)


def first_back_kernel(count, *refs):
    backs, weights, (x, out, terms_out) = refs[: 3 * count], refs[3 * count : -3], refs[-3:]
    grad = None
    for i in range(3):
        back = jnp.concatenate([one[...] for one in backs[i * count : (i + 1) * count]], axis=1)
        term = dot(back, weights[i][...], NT)
        grad = term if grad is None else grad + term
    out[...] = grad.astype(out.dtype)
    shaped, _ = normalize(x[...].astype(F32))

    @pl.when(pl.program_id(0) == 0)
    def _():
        terms_out[...] = jnp.zeros_like(terms_out)

    terms_out[0:1, :] += jnp.sum(grad * shaped, axis=0, keepdims=True)
    terms_out[1:2, :] += jnp.sum(grad, axis=0, keepdims=True)


def first_back(bq, bk, bv, wq, wk, wv, x, kind, after=()):
    rows, width = x.shape
    mine = wq.shape[1]
    count = len(bq)
    block = math.gcd(rows, 256)
    row = lambda cols: pl.BlockSpec((block, cols), lambda i: (i, 0))
    return call(
        functools.partial(first_back_kernel, count),
        (rows // block,),
        [row(mine // count)] * (3 * count) + [whole(width, mine)] * 3 + [row(width)],
        [row(width), whole(2, width)],
        [shape((rows, width), kind), shape((2, width), F32)],
        flops=6 * rows * width * mine,
        name="first_back",
        after=after,
    )(*bq, *bk, *bv, wq, wk, wv, x)


def input_back_kernel(own, other, x, res, gain, out):
    shaped, invert = normalize(x[...].astype(F32))
    grad = own[...] + other[...].astype(F32)
    out[...] = res[...] + norm_back(grad, shaped, invert, gain[...])


def input_back(own, other, x, res, gain, after=()):
    rows, width = x.shape
    block = math.gcd(rows, 128)
    row = pl.BlockSpec((block, width), lambda i: (i, 0))
    return call(
        input_back_kernel,
        (rows // block,),
        [row] * 4 + [whole(1, width)],
        [row],
        [shape((rows, width), F32)],
        name="input_back",
        after=after,
    )(own, other, x, res, gain)[0]


def output_kernel(res, own, other, out):
    out[...] = (res[...] + own[...] + other[...].astype(F32)).astype(out.dtype)


def add_output(res, own, other, after=()):
    rows, width = res.shape
    block = math.gcd(rows, 256)
    row = pl.BlockSpec((block, width), lambda i: (i, 0))
    return call(
        output_kernel,
        (rows // block,),
        [row] * 3,
        [row],
        [shape((rows, width), BF)],
        name="add_output",
        after=after,
    )(res, own, other)[0]


def down_kernel(hidden, weight, out):
    out[...] = dot(hidden[...], weight[...]).astype(out.dtype)


def down_product(hid, wd, after=()):
    rows, width = hid.shape[0], wd.shape[1]
    block = math.gcd(width, 512)
    return call(
        down_kernel,
        (width // block,),
        [whole(*hid.shape), pl.BlockSpec((wd.shape[0], block), lambda j: (0, j))],
        [pl.BlockSpec((rows, block), lambda j: (0, j))],
        [shape((rows, width), BF)],
        flops=2 * rows * width * wd.shape[0],
        name="down_product",
        after=after,
    )(hid, wd)[0]


def pair_swap(values):
    return lax.ppermute(values, "tensor", [(0, 1), (1, 0)])


def dp_swap(values, bit, parts):
    return lax.ppermute(values, "dp", [(i, i ^ (1 << bit)) for i in range(parts)])


def combine_kernel(place, keep0, got0, keep1, got1, keep_out, send_out):
    keep_out[...] = (keep0[...].astype(F32) + got0[...].astype(F32)).astype(BF)
    send_out[...] = (keep1[...].astype(F32) + got1[...].astype(F32)).astype(BF)


def finish_kernel(turn, keep, got, out):
    total = keep[...].astype(F32) + got[...].astype(F32)
    out[...] = total.T if turn else total


class Scatter:
    def __init__(self, keep, send, order, parts, place):
        self.parts, self.place, self.order = parts, place, list(order)
        self.left = list(range(parts.bit_length() - 2, 0, -1)) if parts > 1 else []
        self.keep, self.got = keep, dp_swap(send, 0, parts)

    def advance(self, after=()):
        if not self.order:
            return tuple(after)
        bit = self.order.pop(0)
        axis = self.left.index(bit)
        self.left.remove(bit)
        each, columns = self.keep.shape[-2:]
        high, low = 2**axis, 2 ** (len(self.left) - axis)
        view = (high, 2, low, each, columns)
        block = math.gcd(columns, 2048) if columns % 1024 == 0 else columns
        mine = ((self.place >> bit) & 1).astype(jnp.int32).reshape(1)
        here = pl.BlockSpec((high, None, low, each, block), lambda j, at: (0, at[0], 0, 0, j))
        there = pl.BlockSpec((high, None, low, each, block), lambda j, at: (0, 1 - at[0], 0, 0, j))
        out = pl.BlockSpec((high, low, each, block), lambda j, at: (0, 0, 0, j))
        keep, got = self.keep.reshape(view), self.got.reshape(view)
        self.keep, send = call(
            combine_kernel,
            (columns // block,),
            [here, here, there, there],
            [out, out],
            [shape((high, low, each, columns), BF)] * 2,
            name="combine",
            after=after,
            scalars=1,
        )(mine, keep, got, keep, got)
        self.got = dp_swap(send, bit, self.parts)
        return (self.keep,)

    def finish(self, turn=False, after=()):
        while self.order:
            after = self.advance(after)
        each, columns = self.keep.shape[-2:]
        flat = (each, columns)
        return call(
            functools.partial(finish_kernel, turn),
            (1,),
            [whole(*flat)] * 2,
            [whole(columns, each) if turn else whole(*flat)],
            [shape((columns, each) if turn else flat, F32)],
            name="finish",
            after=after,
        )(self.keep.reshape(flat), self.got.reshape(flat))


def body(
    parts,
    tokens,
    cotangent,
    species,
    wq,
    wk,
    wv,
    wo,
    first_gain,
    first_bias,
    second_gain,
    second_bias,
    wg,
    wu,
    wd,
):
    place = lax.axis_index("dp")
    half = lax.axis_index("tensor")
    core = (place & 1).astype(jnp.int32).reshape(1)
    rows = tokens.shape[0]
    bits = parts.bit_length() - 1
    low_first = list(range(1, bits))
    high_first = list(range(2, bits)) + [1]
    first_gain, first_bias = first_gain[None], first_bias[None]
    second_gain, second_bias = second_gain[None], second_bias[None]

    tokens1 = pair_swap(tokens)
    cot1 = pair_swap(cotangent)
    table0 = rotary_tables(half * rows, rows)
    table1 = rotary_tables((1 - half) * rows, rows)
    first0, q0, k0, v0 = project(tokens, first_gain, first_bias, wq, wk, wv, table0)
    first1, q1, k1, v1 = project(tokens1, first_gain, first_bias, wq, wk, wv, table1)
    mixed1, lse1 = attend(q1, k0, k1, v0, v1)
    attn_got = pair_swap(dot(mixed1, wo).astype(BF))
    mixed0, lse0 = attend(q0, k0, k1, v0, v1, after=(mixed1,))
    gr0, gr1 = scale_rows(species, cotangent, cot1, after=(mixed0,))
    res, second0 = residual(tokens, mixed0, wo, attn_got, second_gain, second_bias, after=(gr0,))
    second1 = pair_swap(second0)
    wo1 = pair_swap(relay(wo, (second0,)))
    hid0, gb0, ub0, st0, ff0 = feed(second0, gr0, wg, wu, wd, F32, True)
    hid1, gb1, ub1, st1 = feed(second1, gr1, wg, wu, wd, BF, False, after=(st0,))

    st_got = pair_swap(st1)
    seconds = [second0, second1]
    gate_keep, gate_send, up_keep, up_send = weight_grad(
        core, parts, [(seconds, [[gb0], [gb1]]), (seconds, [[ub0], [ub1]])], after=(st1,)
    )
    gate = Scatter(gate_keep, gate_send, low_first, parts, place)
    up = Scatter(up_keep, up_send, high_first, parts, place)
    down_keep, down_send = weight_grad(
        core, parts, [([gr0, gr1], [[hid0], [hid1]])], after=(gate_keep, wo1)
    )
    down = Scatter(down_keep, down_send, low_first, parts, place)
    grad_res, attn_grad0, gm0, gm_give, second_terms = res_back(
        species, st0, st_got, cotangent, res, second_gain, wo, wo1, after=(down_keep,)
    )
    gm1 = pair_swap(gm_give)
    attn_grad1 = pair_swap(attn_grad0)
    step = gate.advance(after=(grad_res,))
    step = up.advance(after=step)
    step = down.advance(after=step)

    pairs = q0.shape[1] // PAIR
    back = lambda start, stop, after: attend_back(
        start,
        stop,
        (q0, q1),
        (k0, k1),
        (v0, v1),
        (gm0, gm1),
        (mixed0, mixed1),
        (lse0, lse1),
        (table0[0], table1[0]),
        (table0[1], table1[1]),
        after=after,
    )
    cut = pairs // 2
    firsts = (first0, first1)
    both = lambda i, j: [low[i][j], high[i][j]]
    low = back(0, cut, step)
    step = gate.advance(after=(low[0][0],))
    step = up.advance(after=step)
    low_keep, low_send = head_grad(
        core, parts, firsts, low, out_job=(attn_grad0, attn_grad1, mixed0, mixed1), after=step
    )
    heads0 = Scatter(low_keep, low_send, low_first, parts, place)
    high = back(cut, pairs, (low_keep,))
    step = down.advance(after=(high[0][0],))
    step = gate.advance(after=step)
    step = up.advance(after=step)
    ft1, terms1 = first_back(
        both(0, 1), both(1, 1), both(2, 1), wq, wk, wv, tokens1, BF, after=step
    )
    ft_got = pair_swap(ft1)
    step = heads0.advance(after=(ft1,))
    ft0, terms0 = first_back(
        both(0, 0), both(1, 0), both(2, 0), wq, wk, wv, tokens, F32, after=step
    )
    high_keep, high_send = head_grad(
        core, parts, firsts, high, terms=(terms0, terms1, second_terms), after=(ft0,)
    )
    heads1 = Scatter(high_keep, high_send, high_first, parts, place)
    step = down.advance(after=(high_keep,))
    gate_sum = gate.finish(after=step)
    up_sum = up.finish(after=gate_sum)
    step = heads1.advance(after=up_sum)
    ff1 = down_product(hid1, wd, after=step)
    ff_got = pair_swap(ff1)
    step = heads0.advance(after=(ff1,))
    input_grad = input_back(ft0, ft_got, tokens, grad_res, first_gain, after=step)
    down_sum = down.finish(turn=True, after=(input_grad,))
    step = heads1.advance(after=down_sum)
    step = heads0.advance(after=step)
    step = heads1.advance(after=step)
    output = add_output(res, ff0, ff_got, after=step)
    (sum0,) = heads0.finish(after=(output,))
    (sum1,) = heads1.finish(after=(sum0,))

    mine = wq.shape[1]
    low_part, high_part = cut * PAIR, mine - cut * PAIR
    query_sum, key_sum, value_sum = (
        jnp.concatenate(
            [
                sum0[:, i * low_part : (i + 1) * low_part],
                sum1[:, i * high_part : (i + 1) * high_part],
            ],
            axis=1,
        )
        for i in range(3)
    )
    at = 3 * low_part
    out_sum = sum0[:, at : at + mine]
    norm_local = sum1[:, 3 * high_part : 3 * high_part + 4]
    norm_local = norm_local + pair_swap(norm_local)
    return (
        output,
        input_grad,
        query_sum,
        key_sum,
        value_sum,
        out_sum.T,
        gate_sum[0],
        up_sum[0],
        down_sum[0],
        norm_local.T,
    )


def solution(mesh):
    in_specs = (
        P(("dp", "tensor"), None),
        P(("dp", "tensor"), None),
        P("dp"),
        P(None, "tensor"),
        P(None, "tensor"),
        P(None, "tensor"),
        P("tensor", None),
        P(),
        P(),
        P(),
        P(),
        P(None, "tensor"),
        P(None, "tensor"),
        P("tensor", None),
    )
    out_specs = (
        P(("dp", "tensor"), None),
        P(("dp", "tensor"), None),
        P("dp", "tensor"),
        P("dp", "tensor"),
        P("dp", "tensor"),
        P("tensor", "dp"),
        P("dp", "tensor"),
        P("dp", "tensor"),
        P("tensor", "dp"),
        P(None, "dp"),
    )
    return jax.shard_map(
        functools.partial(body, mesh.shape["dp"]),
        mesh=mesh,
        in_specs=in_specs,
        out_specs=out_specs,
        check_vma=False,
    )
```

```python
import functools
import math

import jax
import jax.numpy as jnp
from jax import lax
from jax.experimental import pallas as pl
from jax.experimental.pallas import tpu as pltpu
from jax.sharding import PartitionSpec as P

HEAD_DIM = 64
PAIR = 2 * HEAD_DIM
EPS = 1e-05
BASE = 10000.0
BF = jnp.bfloat16
F32 = jnp.float32
MOST = 60 * 1024 * 1024
COST = 1000

NN = (((1,), (0,)), ((), ()))
NT = (((1,), (1,)), ((), ()))


def dot(left, right, dims=NN):
    return lax.dot_general(left, right, dims, preferred_element_type=F32)


def shape(dims, kind):
    return jax.ShapeDtypeStruct(dims, kind)


def call(
    kernel,
    grid,
    in_specs,
    out_specs,
    out_shape,
    scratch=(),
    flops=0,
    name=None,
    after=(),
    scalars=0,
    limit=MOST,
):
    count = len(after)
    moved = sum(math.prod(s.shape) * s.dtype.itemsize for s in out_shape)

    def ordered(*refs):
        given = scalars + len(in_specs)
        kernel(*refs[:given], *refs[given + count :])

    made = pl.pallas_call(
        ordered,
        grid_spec=pltpu.PrefetchScalarGridSpec(
            num_scalar_prefetch=scalars,
            grid=grid,
            in_specs=list(in_specs) + [pl.BlockSpec(memory_space=pl.ANY)] * count,
            out_specs=out_specs,
            scratch_shapes=scratch,
        ),
        out_shape=out_shape,
        compiler_params=pltpu.CompilerParams(vmem_limit_bytes=limit),
        cost_estimate=pl.CostEstimate(
            flops=int(flops + 3e9) * COST, bytes_accessed=2 * moved, transcendentals=0
        ),
        name=name,
    )
    return lambda *given: made(*given, *after)


SMEM = pl.BlockSpec(memory_space=pltpu.SMEM)


def whole(*dims):
    return pl.BlockSpec(dims, lambda *at: (0,) * len(dims))


def normalize(rows):
    center = rows - jnp.mean(rows, axis=-1, keepdims=True)
    invert = lax.rsqrt(jnp.mean(center * center, axis=-1, keepdims=True) + EPS)
    return center * invert, invert


def norm_back(grad, shaped, invert, gain):
    inner = grad * gain
    return invert * (
        inner
        - jnp.mean(inner, axis=-1, keepdims=True)
        - shaped * jnp.mean(inner * shaped, axis=-1, keepdims=True)
    )


def lower_half(width):
    lane = lax.broadcasted_iota(jnp.int32, (1, width), 1)
    return (lane % HEAD_DIM) < HEAD_DIM // 2


def swap_halves(values):
    width = values.shape[-1]
    half = HEAD_DIM // 2
    return jnp.where(
        lower_half(width), pltpu.roll(values, width - half, 1), pltpu.roll(values, half, 1)
    )


def rotate(values, cosine, sine):
    turned = swap_halves(values)
    return values * cosine + jnp.where(lower_half(values.shape[-1]), -turned, turned) * sine


def unrotate(grad, cosine, sine):
    turned = swap_halves(grad * sine)
    return grad * cosine + jnp.where(lower_half(grad.shape[-1]), turned, -turned)


def rotary_tables(start, length):
    half = HEAD_DIM // 2
    freq = BASE ** (-(jnp.arange(half, dtype=F32) * 2.0 / HEAD_DIM))
    place = (start + jnp.arange(length, dtype=jnp.int32)).astype(F32)
    angle = place[:, None] * jnp.concatenate([freq] * (PAIR // half))[None, :]
    return jnp.cos(angle), jnp.sin(angle)


def project_kernel(scale, x, gain, bias, wq, wk, wv, cos, sin, first_out, q_out, k_out, v_out):
    shaped, _ = normalize(x[...].astype(F32))
    first = (shaped * gain[...] + bias[...]).astype(BF)
    first_out[...] = first
    cosine, sine = cos[...], sin[...]
    for weight, out, factor in ((wq, q_out, scale), (wk, k_out, 1.0)):
        made = dot(first, weight[...])
        for at in range(0, made.shape[1], PAIR):
            turned = rotate(made[:, at : at + PAIR], cosine, sine).astype(BF)
            out[:, at : at + PAIR] = turned * factor if factor != 1.0 else turned
    v_out[...] = dot(first, wv[...]).astype(BF)


def project(x, gain, bias, wq, wk, wv, tables, after=()):
    rows, width = x.shape
    mine = wq.shape[1]
    block = math.gcd(rows, 256)
    row = lambda cols: pl.BlockSpec((block, cols), lambda i: (i, 0))
    scale = HEAD_DIM ** (-0.5)
    return call(
        functools.partial(project_kernel, scale),
        (rows // block,),
        [row(width), whole(1, width), whole(1, width)]
        + [whole(width, mine)] * 3
        + [row(PAIR), row(PAIR)],
        [row(width), row(mine), row(mine), row(mine)],
        [shape((rows, width), BF)] + [shape((rows, mine), BF)] * 3,
        flops=6 * rows * width * mine,
        name="project",
        after=after,
    )(x, gain, bias, wq, wk, wv, *tables)


def attend_kernel(block, q, k0, k1, v0, v1, out, lse):
    lane = lax.broadcasted_iota(jnp.int32, (1, PAIR), 1)
    keys = jnp.concatenate([k0[...], k1[...]], axis=0)
    length = keys.shape[0]
    ones = jnp.where(lax.broadcasted_iota(jnp.int32, (length, PAIR), 1) == 0, 1.0, 0.0).astype(BF)
    values = jnp.concatenate([jnp.concatenate([v0[...], v1[...]], axis=0), ones], axis=1)
    for at in range(0, q.shape[0], block):
        rows = q[at : at + block, :]
        mixed = []
        for head in range(2):
            own = jnp.where((lane // HEAD_DIM) == head, rows, jnp.zeros_like(rows))
            scores = dot(own, keys, NT)
            top = jnp.max(scores, axis=-1, keepdims=True)
            probs = jnp.exp(scores - top).astype(BF)
            summed = dot(probs, values)
            total = summed[:, PAIR : PAIR + 1]
            mixed.append(summed[:, :PAIR] / total)
            lse[0, head, at : at + block] = (top + jnp.log(total))[:, 0]
        out[at : at + block, :] = jnp.where(lane < HEAD_DIM, mixed[0], mixed[1]).astype(BF)


def attend(q, k0, k1, v0, v1, after=()):
    rows, mine = q.shape
    pairs = mine // PAIR
    column = pl.BlockSpec((rows, PAIR), lambda i: (0, i))
    return call(
        functools.partial(attend_kernel, math.gcd(rows, 128)),
        (pairs,),
        [column] * 5,
        [column, pl.BlockSpec((1, 2, rows), lambda i: (i, 0, 0))],
        [shape((rows, mine), BF), shape((pairs, 2, rows), F32)],
        flops=16 * rows * rows * mine,
        name="attend",
        after=after,
    )(q, k0, k1, v0, v1)


def attend_back_kernel(block, *refs):
    (q, k, v, g, o, lse, cos, sin), outs = (
        [refs[2 * i : 2 * i + 2] for i in range(8)],
        refs[16:22],
    )
    dq, dk, dv = outs[0:2], outs[2:4], outs[4:6]
    key_acc, value_acc = refs[22:24]
    lane = lax.broadcasted_iota(jnp.int32, (1, PAIR), 1)
    keys = jnp.concatenate([k[0][...], k[1][...]], axis=0)
    values = jnp.concatenate([v[0][...], v[1][...]], axis=0)
    keys_t = keys.T
    rows = q[0].shape[0]
    scale = HEAD_DIM ** (-0.5)
    started = False
    for part in range(2):
        for at in range(0, rows, block):
            span = slice(at, at + block)
            query, grad = q[part][span, :], g[part][span, :]
            weighed = (grad.astype(F32) * o[part][span, :].astype(F32)).T
            key_sum, value_sum, query_back = None, None, []
            for head in range(2):
                mine = (lane // HEAD_DIM) == head
                own = jnp.where(mine, query, jnp.zeros_like(query))
                own_grad = jnp.where(mine, grad, jnp.zeros_like(grad))
                head_rows = slice(head * HEAD_DIM, (head + 1) * HEAD_DIM)
                delta = jnp.sum(weighed[head_rows, :], axis=0, keepdims=True)
                probs = jnp.exp(dot(keys, own, NT) - lse[part][0, head : head + 1, span])
                grad_scores = (probs * (dot(values, own_grad, NT) - delta)).astype(BF)
                value_one = dot(probs.astype(BF), own_grad)
                key_one = dot(grad_scores, own)
                query_back.append(dot(keys_t[head_rows, :], grad_scores))
                key_sum = key_one if key_sum is None else key_sum + key_one
                value_sum = value_one if value_sum is None else value_sum + value_one
            if started:
                key_acc[...] += key_sum
                value_acc[...] += value_sum
            else:
                key_acc[...] = key_sum
                value_acc[...] = value_sum
                started = True
            back = jnp.concatenate(query_back, axis=0).T * scale
            dq[part][span, :] = unrotate(back, cos[part][span, :], sin[part][span, :]).astype(BF)
    for part in range(2):
        span = slice(part * rows, (part + 1) * rows)
        dk[part][...] = unrotate(key_acc[span, :], cos[part][...], sin[part][...]).astype(BF)
        dv[part][...] = value_acc[span, :].astype(BF)


def attend_back(start, stop, q, k, v, g, o, lse, cos, sin, after=()):
    rows = q[0].shape[0]
    pairs = stop - start
    mine = pairs * PAIR
    column = pl.BlockSpec((rows, PAIR), lambda i: (0, start + i))
    made = pl.BlockSpec((rows, PAIR), lambda i: (0, i))
    stat = pl.BlockSpec((1, 2, rows), lambda i: (start + i, 0, 0))
    table = whole(rows, PAIR)
    outs = call(
        functools.partial(attend_back_kernel, math.gcd(rows, 256)),
        (pairs,),
        [column] * 10 + [stat] * 2 + [table] * 4,
        [made] * 6,
        [shape((rows, mine), BF)] * 6,
        scratch=[pltpu.VMEM((2 * rows, PAIR), F32)] * 2,
        flops=80 * rows * rows * mine,
        name="attend_back",
        after=after,
    )(*q, *k, *v, *g, *o, *lse, *cos, *sin)
    return outs[0:2], outs[2:4], outs[4:6]


def residual_kernel(x, mixed, weight, other, gain, bias, res_out, second_out, *passed):
    for out in passed:
        out[...] = weight[...]
    res = x[...].astype(F32) + dot(mixed[...], weight[...]) + other[...].astype(F32)
    res_out[...] = res
    shaped, _ = normalize(res)
    second_out[...] = (shaped * gain[...] + bias[...]).astype(BF)


def residual(start, rows, x, mixed, weight, other, gain, bias, more, after=()):
    width = x.shape[1]
    mine = mixed.shape[1]
    block = math.gcd(rows, 256)
    row = lambda cols: pl.BlockSpec((block, cols), lambda i: (start // block + i, 0))
    own = pl.BlockSpec((block, width), lambda i: (i, 0))
    return call(
        residual_kernel,
        (rows // block,),
        [row(width), row(mine), whole(mine, width), own, whole(1, width), whole(1, width)],
        [own, own] + [whole(mine, width)] * more,
        [shape((rows, width), F32), shape((rows, width), BF)]
        + [shape((mine, width), BF)] * more,
        flops=2 * rows * width * mine,
        name="residual",
        after=after,
    )(x, mixed, weight, other, gain, bias)


def product_kernel(left, right, out):
    out[...] = dot(left[...], right[...]).astype(out.dtype)


def halves_kernel(left, right, out0, out1):
    cut = out0.shape[0]
    out0[...] = dot(left[:cut, :], right[...]).astype(out0.dtype)
    out1[...] = dot(left[cut:, :], right[...]).astype(out1.dtype)


def product_halves(left, right, after=()):
    rows, width = left.shape[0] // 2, right.shape[1]
    return call(
        halves_kernel,
        (1,),
        [whole(*left.shape), whole(*right.shape)],
        [whole(rows, width)] * 2,
        [shape((rows, width), BF)] * 2,
        flops=4 * rows * left.shape[1] * width,
        name="product_halves",
        after=after,
    )(left, right)


def down_product(hid, wd, after=()):
    rows, width = hid.shape[0], wd.shape[1]
    block = math.gcd(width, 512)
    return call(
        product_kernel,
        (width // block,),
        [whole(*hid.shape), pl.BlockSpec((wd.shape[0], block), lambda j: (0, j))],
        [pl.BlockSpec((rows, block), lambda j: (0, j))],
        [shape((rows, width), BF)],
        flops=2 * rows * width * wd.shape[0],
        name="down_product",
        after=after,
    )(hid, wd)[0]


def scale_kernel(species, cot, weight, rows_out, hidden_out):
    @pl.when(pl.program_id(0) == 0)
    def _():
        rows_out[...] = (cot[...].astype(F32) * species[0].astype(F32)).astype(BF)

    hidden_out[...] = dot(rows_out[...], weight[...], NT)


def scale_rows(species, cot, weight, after=()):
    rows, width = cot.shape
    hidden = weight.shape[0]
    block = math.gcd(hidden, 512)
    return call(
        scale_kernel,
        (hidden // block,),
        [SMEM, whole(rows, width), pl.BlockSpec((block, width), lambda j: (j, 0))],
        [whole(rows, width), pl.BlockSpec((rows, block), lambda j: (0, j))],
        [shape((rows, width), BF), shape((rows, hidden), F32)],
        flops=2 * rows * width * hidden,
        name="scale_rows",
        after=after,
    )(species, cot, weight)


def feed_kernel(count, forward, *refs):
    seconds, (grad_hidden, wg, wu), refs = refs[:count], refs[count : count + 3], refs[count + 3 :]
    if forward:
        wd, refs = refs[0], refs[1:]
    hid_out, gb_out, ub_out, refs = *refs[:3], refs[3:]
    outs, accs = refs[: 1 + forward], refs[1 + forward :]
    step = pl.program_id(0)
    rows = jnp.concatenate([one[...] for one in seconds], axis=0)
    gate = dot(rows, wg[...])
    upper = dot(rows, wu[...])
    grad_hidden = grad_hidden[...]
    sigma = 0.5 * jnp.tanh(0.5 * gate) + 0.5
    active = gate * sigma
    hidden = (active * upper).astype(BF)
    gate_back = (grad_hidden * upper * (sigma + active * (1.0 - sigma))).astype(BF)
    up_back = (grad_hidden * active).astype(BF)
    hid_out[...] = hidden
    gb_out[...] = gate_back
    ub_out[...] = up_back
    terms = [dot(gate_back, wg[...], NT) + dot(up_back, wu[...], NT)]
    if forward:
        terms.append(dot(hidden, wd[...]))

    @pl.when(step == 0)
    def _():
        for acc, term in zip(accs, terms):
            acc[...] = term

    @pl.when(step > 0)
    def _():
        for acc, term in zip(accs, terms):
            acc[...] += term

    @pl.when(step == pl.num_programs(0) - 1)
    def _():
        for out, acc in zip(outs, accs):
            out[...] = acc[...].astype(out.dtype)


def feed(seconds, grad_hidden, wg, wu, kind, wd=None, after=()):
    rows = sum(one.shape[0] for one in seconds)
    width, hidden = wg.shape
    block = math.gcd(hidden, 512)
    column = pl.BlockSpec((width, block), lambda j: (0, j))
    wide = pl.BlockSpec((rows, block), lambda j: (0, j))
    forward = wd is not None
    more = [wd] if forward else []
    return call(
        functools.partial(feed_kernel, len(seconds), int(forward)),
        (hidden // block,),
        [whole(*one.shape) for one in seconds]
        + [wide, column, column]
        + [pl.BlockSpec((block, width), lambda j: (j, 0))] * forward,
        [wide, wide, wide] + [whole(rows, width)] * (1 + forward),
        [shape((rows, hidden), BF)] * 3 + [shape((rows, width), kind)] * (1 + forward),
        scratch=[pltpu.VMEM((rows, width), F32)] * (1 + forward),
        flops=12 * rows * width * hidden,
        name="feed",
        after=after,
    )(*seconds, grad_hidden, wg, wu, *more)


def flip(out, parts):
    at = 0
    for part in parts:
        rows = part.shape[0]
        out[:, at : at + rows] = part[...].T
        at += rows


def give_out(own, keep, send, span, value):
    value = value.reshape(keep.shape[0], 2, keep.shape[1], value.shape[1])
    even, odd = value[:, 0], value[:, 1]
    keep[:, :, span] = jnp.where(own == 1, odd, even).astype(BF)
    send[:, :, span] = jnp.where(own == 1, even, odd).astype(BF)


def weight_grad_kernel(jobs, core, *refs):
    outs, flipped = refs[-1 - 2 * len(jobs) : -1], refs[-1]
    step = pl.program_id(0)
    at = 0
    for keep, send, (count, pieces, steps, fresh) in zip(outs[::2], outs[1::2], jobs):
        left, refs = refs[:count], refs[count:]
        right, refs = refs[:pieces], refs[pieces:]
        rows = sum(one.shape[0] for one in left)

        if fresh:

            @pl.when(step == at)
            def _():
                flip(flipped, left)

        @pl.when((step >= at) & (step < at + steps))
        def _():
            value = dot(flipped[:, :rows], jnp.concatenate([one[...] for one in right], axis=0))
            give_out(core[0], keep, send, slice(None), value)

        at += steps


def weight_grad(core, parts, jobs, after=()):
    width = jobs[0][0][0].shape[1]
    each = width // parts
    kinds, specs, given, outs, kept, at, most, last_left = [], [], [], [], [], 0, 0, None
    for left, right in jobs:
        wide = right[0].shape[1]
        block = math.gcd(wide, 1024)
        steps = wide // block
        most = max(most, sum(one.shape[0] for one in left))
        column = lambda j, at=at, last=steps - 1: jnp.clip(j - at, 0, last)
        specs += [whole(*one.shape) for one in left]
        specs += [
            pl.BlockSpec((one.shape[0], block), lambda j, column=column: (0, column(j)))
            for one in right
        ]
        given += [*left, *right]
        outs += [
            pl.BlockSpec((parts // 2, each, block), lambda j, column=column: (0, 0, column(j)))
        ] * 2
        kept += [shape((parts // 2, each, wide), BF)] * 2
        kinds.append((len(left), len(right), steps, left is not last_left))
        last_left = left
        at += steps
    return call(
        functools.partial(weight_grad_kernel, kinds),
        (at,),
        [SMEM] + specs,
        outs,
        kept,
        scratch=[pltpu.VMEM((width, most), BF)],
        flops=2 * most * width * sum(job[1][0].shape[1] for job in jobs),
        name="weight_grad",
        after=after,
    )(core, *given)


def head_grad_kernel(count, with_out, core, *refs):
    first, backs, refs = refs[:2], refs[2 : 2 + 2 * count], refs[2 + 2 * count :]
    keep, send, flipped = refs[-3:]
    flip(flipped, first)
    at = 0
    for i in range(count):
        right = jnp.concatenate([backs[2 * i][...], backs[2 * i + 1][...]], axis=0)
        wide = right.shape[1]
        give_out(core[0], keep, send, slice(at, at + wide), dot(flipped[...], right))
        at += wide
    if with_out:
        flip(flipped, refs[0:2])
        right = jnp.concatenate([refs[2][...], refs[3][...]], axis=0)
        give_out(core[0], keep, send, slice(at, at + right.shape[1]), dot(flipped[...], right))
    else:
        rows = [refs[0][...] + refs[1][...]]
        rows.append(jnp.zeros((PAIR - 4, rows[0].shape[1]), F32))
        value = jnp.concatenate(rows, axis=0).T
        give_out(core[0], keep, send, slice(at, at + PAIR), value)


def head_grad(core, parts, first, backs, out_job=(), terms=(), after=()):
    rows, width = first[0].shape
    each = width // parts
    total = sum(back[0].shape[1] for back in backs)
    total += out_job[2].shape[1] if out_job else PAIR
    given = [*first, *[half for pair in backs for half in pair], *out_job, *terms]
    out = whole(parts // 2, each, total)
    return call(
        functools.partial(head_grad_kernel, len(backs), bool(out_job)),
        (1,),
        [SMEM] + [whole(*one.shape) for one in given],
        [out] * 2,
        [shape((parts // 2, each, total), BF)] * 2,
        scratch=[pltpu.VMEM((width, 2 * rows), BF)],
        flops=4 * rows * width * total,
        name="head_grad",
        after=after,
    )(core, *given)


def res_back_kernel(
    species, own, other, cot, res0, res1, gain, w0, w1, *outs
):
    grad_out, attn_out, gm0_out, gm1_out, terms_out = outs
    res = jnp.where(pl.program_id(0) == 0, res0[...], res1[...])
    grad = own[...] + other[...].astype(F32)
    shaped, invert = normalize(res)
    made = cot[...].astype(F32) * species[0].astype(F32) + norm_back(
        grad, shaped, invert, gain[...]
    )
    grad_out[...] = made
    attn = made.astype(BF)
    attn_out[...] = attn
    gm1_out[...] = dot(attn, w1[...], NT).astype(BF)
    gm0_out[...] = dot(attn, w0[...], NT).astype(BF)

    @pl.when(pl.program_id(0) == 0)
    def _():
        terms_out[...] = jnp.zeros_like(terms_out)

    terms_out[0:1, :] += jnp.sum(grad * shaped, axis=0, keepdims=True)
    terms_out[1:2, :] += jnp.sum(grad, axis=0, keepdims=True)


def res_back(species, own, other, cot, res, gain, w0, w1, after=()):
    rows, width = own.shape
    mine = w0.shape[0]
    block = rows // 2
    row = lambda cols: pl.BlockSpec((block, cols), lambda i: (i, 0))
    return call(
        res_back_kernel,
        (rows // block,),
        [SMEM] + [row(width)] * 3 + [whole(block, width)] * 2
        + [whole(1, width)] + [whole(mine, width)] * 2,
        [row(width), row(width), row(mine), row(mine), whole(2, width)],
        [
            shape((rows, width), F32),
            shape((rows, width), BF),
            shape((rows, mine), BF),
            shape((rows, mine), BF),
            shape((2, width), F32),
        ],
        flops=4 * rows * width * mine,
        name="res_back",
        after=after,
    )(species, own, other, cot, *res, gain, w0, w1)


def first_back_kernel(count, half, *refs):
    sides, refs = (refs[: 3 * count], refs[3 * count : 6 * count]), refs[6 * count :]
    weights, tokens, (more, out1, out0, terms_out) = refs[:3], refs[3:5], refs[5:]

    @pl.when(pl.program_id(0) == 0)
    def _():
        terms_out[0:2, :] = jnp.zeros_like(more)
        terms_out[2:4, :] = more[...]

    for side, (backs, x, out) in enumerate(zip(sides, tokens, (out1, out0))):

        @pl.when(within(pl.program_id(0), side * half, half))
        def _():
            grad = None
            for i in range(3):
                beside = [one[...] for one in backs[i * count : (i + 1) * count]]
                term = dot(jnp.concatenate(beside, axis=1), weights[i][...], NT)
                grad = term if grad is None else grad + term
            out[...] = grad.astype(out.dtype)
            shaped, _ = normalize(x[...].astype(F32))
            terms_out[0:1, :] += jnp.sum(grad * shaped, axis=0, keepdims=True)
            terms_out[1:2, :] += jnp.sum(grad, axis=0, keepdims=True)


def first_back(groups, wq, wk, wv, tokens, terms, after=()):
    rows, width = tokens[0].shape
    mine = wq.shape[1]
    count = len(groups)
    block = math.gcd(rows, 256)
    half = rows // block
    given, specs = [], []
    for side in (1, 0):
        at = half * (1 - side)
        place = lambda i, at=at: (jnp.clip(i - at, 0, half - 1), 0)
        for kind in range(3):
            for group in groups:
                given.append(group[kind][side])
                specs.append(pl.BlockSpec((block, given[-1].shape[1]), place))
    outs = [
        pl.BlockSpec((block, width), lambda i, at=at: (jnp.clip(i - at, 0, half - 1), 0))
        for at in (0, half)
    ]
    return call(
        functools.partial(first_back_kernel, count, half),
        (2 * half,),
        specs + [whole(width, mine)] * 3 + outs + [whole(2, width)],
        outs + [whole(4, width)],
        [shape((rows, width), BF), shape((rows, width), F32), shape((4, width), F32)],
        flops=12 * rows * width * mine,
        name="first_back",
        after=after,
    )(*given, wq, wk, wv, tokens[1], tokens[0], terms)


def input_back_kernel(own, other, x, res, gain, out):
    shaped, invert = normalize(x[...].astype(F32))
    grad = own[...] + other[...].astype(F32)
    out[...] = res[...] + norm_back(grad, shaped, invert, gain[...])


def input_back(own, other, x, res, gain, after=()):
    rows, width = x.shape
    block = math.gcd(rows, 128)
    row = pl.BlockSpec((block, width), lambda i: (i, 0))
    return call(
        input_back_kernel,
        (rows // block,),
        [row] * 4 + [whole(1, width)],
        [row],
        [shape((rows, width), F32)],
        name="input_back",
        after=after,
    )(own, other, x, res, gain)[0]


def output_kernel(res0, res1, own, other, out):
    res = jnp.where(pl.program_id(0) == 0, res0[...], res1[...])
    out[...] = (res + own[...] + other[...].astype(F32)).astype(out.dtype)


def add_output(res, own, other, after=()):
    rows, width = own.shape
    block = rows // 2
    row = pl.BlockSpec((block, width), lambda i: (i, 0))
    return call(
        output_kernel,
        (2,),
        [whole(block, width)] * 2 + [row] * 2,
        [row],
        [shape((rows, width), BF)],
        name="add_output",
        after=after,
    )(*res, own, other)[0]


def pair_swap(values):
    return lax.ppermute(values, "tensor", [(0, 1), (1, 0)])


def dp_swap(values, turn, parts):
    return lax.ppermute(values, "dp", [(i, i ^ turn) for i in range(parts)])


def within(step, start, steps):
    return (step >= start) & (step < start + steps)


def total_of(refs):
    total = refs[0][...].astype(F32)
    for one in refs[1:]:
        total = total + one[...].astype(F32)
    return total


def combine_kernel(spans, places, *refs):
    count = sum(terms * shares for _, _, terms, shares in spans)
    ins, outs = refs[:count], refs[count:]
    for start, steps, terms, shares in spans:
        given, ins = ins[: terms * shares], ins[terms * shares :]
        made, outs = outs[:shares], outs[shares:]

        @pl.when(within(pl.program_id(0), start, steps))
        def _():
            for r in range(shares):
                made[r][...] = total_of(given[r * terms : (r + 1) * terms]).astype(BF)


class Scatter:
    def __init__(self, keep, send, order, count, place):
        self.count, self.place, self.order = count, place, list(order)
        self.left = list(range(count.bit_length() - 2, 0, -1))
        self.parts = [keep, dp_swap(send, 1, count)]


def advance(chains, after=()):
    chains = [chain for chain in chains if chain.order]
    if not chains:
        return tuple(after)
    spans, places, given, ins, outs, shapes, begin = [], [], [], [], [], [], 0
    for i, chain in enumerate(chains):
        bits = chain.order.pop(0)
        shares = 2 ** len(bits)
        axis = chain.left.index(bits[-1])
        for bit in bits:
            chain.left.remove(bit)
        each, columns = chain.parts[0].shape[-2:]
        high, low = 2**axis, 2 ** (len(chain.left) - axis)
        view = (high, shares, low, each, columns)
        block = 1024 if columns % 1024 == 0 else columns
        last = columns // block - 1
        block_of = lambda j, begin=begin, last=last: jnp.clip(j - begin, 0, last)
        for r in range(shares):
            share = pl.BlockSpec(
                (high, None, low, each, block),
                lambda j, at, i=i, r=r, block_of=block_of: (0, at[i] ^ r, 0, 0, block_of(j)),
            )
            ins += [share] * len(chain.parts)
            given += [one.reshape(view) for one in chain.parts]
        out = pl.BlockSpec(
            (high, low, each, block), lambda j, at, block_of=block_of: (0, 0, 0, block_of(j))
        )
        outs += [out] * shares
        shapes += [shape((high, low, each, columns), BF)] * shares
        spans.append((begin, last + 1, len(chain.parts), shares))
        places.append((chain.place >> bits[0]) & (shares - 1))
        chain.bits, chain.shares = bits, shares
        begin += last + 1
    made = call(
        functools.partial(combine_kernel, spans),
        (begin,),
        ins,
        outs,
        shapes,
        name="combine",
        after=after,
        scalars=1,
    )(jnp.stack(places).astype(jnp.int32), *given)
    first = made[0]
    for chain in chains:
        own, made = made[: chain.shares], made[chain.shares :]
        chain.parts = [own[0]] + [
            dp_swap(own[r], r << chain.bits[0], chain.count) for r in range(1, chain.shares)
        ]
    return (first,)


def finish_kernel(counts, cuts, *refs):
    total = sum(counts)
    ins, outs = refs[:total], refs[total:]
    for count, cut in zip(counts, cuts):
        given, ins = ins[:count], ins[count:]
        value = total_of(given)
        for at, wide, to in cut:
            out, low = outs[to[0]], to[1]
            out[:, low : low + wide] = value[:, at : at + wide]


def finish(chains, cuts, columns, after=()):
    while any(chain.order for chain in chains):
        after = advance(chains, after)
    given, counts = [], []
    for chain in chains:
        flat = chain.parts[0].shape[-2:]
        counts.append(len(chain.parts))
        given += [one.reshape(flat) for one in chain.parts]
    rows = given[0].shape[0]
    return call(
        functools.partial(finish_kernel, counts, cuts),
        (1,),
        [whole(*one.shape) for one in given],
        [whole(rows, wide) for wide in columns],
        [shape((rows, wide), F32) for wide in columns],
        name="finish",
        after=after,
    )(*given)


def body(
    parts,
    tokens,
    cotangent,
    species,
    wq,
    wk,
    wv,
    wo,
    first_gain,
    first_bias,
    second_gain,
    second_bias,
    wg,
    wu,
    wd,
):
    place = lax.axis_index("dp")
    half = lax.axis_index("tensor")
    core = (place & 1).astype(jnp.int32).reshape(1)
    rows = tokens.shape[0]
    bits = parts.bit_length() - 1
    wide = [[bit] for bit in range(2, bits)]
    low_first = [[1]] * (bits > 1) + wide
    high_first = wide + [[1]] * (bits > 1)
    first_gain, first_bias = first_gain[None], first_bias[None]
    second_gain, second_bias = second_gain[None], second_bias[None]

    tokens1 = pair_swap(tokens)
    cot1 = pair_swap(cotangent)
    table0 = rotary_tables(half * rows, rows)
    table1 = rotary_tables((1 - half) * rows, rows)
    first0, q0, k0, v0 = project(tokens, first_gain, first_bias, wq, wk, wv, table0)
    gr0, grad_hidden0 = scale_rows(species, cotangent, wd, after=(first0,))
    first1, q1, k1, v1 = project(
        tokens1, first_gain, first_bias, wq, wk, wv, table1, after=(gr0,)
    )
    mixed1, lse1 = attend(q1, k0, k1, v0, v1)
    cut = rows // 2
    attn_a, attn_b = product_halves(mixed1, wo)
    got_a, got_b = pair_swap(attn_a), pair_swap(attn_b)
    mixed0, lse0 = attend(q0, k0, k1, v0, v1, after=(attn_b,))
    gr1, grad_hidden1 = scale_rows(species, cot1, wd, after=(mixed0,))
    second = lambda start, got, more, after: residual(
        start, cut, tokens, mixed0, wo, got, second_gain, second_bias, more, after=after
    )
    res_a, second0a = second(0, got_a, 0, (grad_hidden1,))
    res_b, second0b, wo_late = second(cut, got_b, 1, (res_a,))
    res = (res_a, res_b)
    second1a, second1b = pair_swap(second0a), pair_swap(second0b)
    wo1 = pair_swap(wo_late)
    hid0, gb0, ub0, st0, ff0 = feed((second0a, second0b), grad_hidden0, wg, wu, F32, wd)
    hid1, gb1, ub1, st1 = feed((second1a, second1b), grad_hidden1, wg, wu, BF, after=(st0,))

    st_got = pair_swap(st1)
    seconds = [second0a, second0b, second1a, second1b]
    gate_keep, gate_send, up_keep, up_send = weight_grad(
        core, parts, [(seconds, [gb0, gb1]), (seconds, [ub0, ub1])], after=(st1,)
    )
    gate = Scatter(gate_keep, gate_send, low_first, parts, place)
    up = Scatter(up_keep, up_send, high_first, parts, place)
    down_keep, down_send = weight_grad(
        core, parts, [([gr0, gr1], [hid0, hid1])], after=(gate_keep, wo1)
    )
    down = Scatter(down_keep, down_send, low_first, parts, place)
    grad_res, attn_grad0, gm0, gm_give, second_terms = res_back(
        species, st0, st_got, cotangent, res, second_gain, wo, wo1, after=(down_keep,)
    )
    gm1 = pair_swap(gm_give)
    attn_grad1 = pair_swap(attn_grad0)
    step = advance([gate], after=(grad_res,))
    step = advance([up], after=step)
    step = advance([down], after=step)

    pairs = q0.shape[1] // PAIR
    back = lambda start, stop, after: attend_back(
        start,
        stop,
        (q0, q1),
        (k0, k1),
        (v0, v1),
        (gm0, gm1),
        (mixed0, mixed1),
        (lse0, lse1),
        (table0[0], table1[0]),
        (table0[1], table1[1]),
        after=after,
    )
    cut = pairs // 2
    firsts = (first0, first1)
    low = back(0, cut, step)
    step = advance([gate], after=(low[0][0],))
    step = advance([up], after=step)
    low_keep, low_send = head_grad(
        core, parts, firsts, low, out_job=(attn_grad0, attn_grad1, mixed0, mixed1), after=step
    )
    heads0 = Scatter(low_keep, low_send, low_first, parts, place)
    high = back(cut, pairs, (low_keep,))
    step = advance([down], after=(high[0][0],))
    step = advance([gate], after=step)
    step = advance([up], after=step)
    ft1, ft0, terms = first_back(
        (low, high), wq, wk, wv, (tokens, tokens1), second_terms, after=step
    )
    terms_got = pair_swap(terms)
    ft_got = pair_swap(ft1)
    step = advance([heads0], after=(ft1,))
    step = advance([down], after=(*step, *gate.parts, *up.parts))
    high_keep, high_send = head_grad(
        core, parts, firsts, high, terms=(terms, terms_got), after=step
    )
    heads1 = Scatter(high_keep, high_send, low_first, parts, place)
    step = advance([heads0], after=(high_keep,))
    step = advance([heads1], after=step)
    hidden = wg.shape[1]
    all_of = lambda to: [(0, hidden, (to, 0))]
    gate_sum, up_sum = finish([gate, up], [all_of(0), all_of(1)], [hidden] * 2, after=step)
    ff1 = down_product(hid1, wd, after=(gate_sum,))
    ff_got = pair_swap(ff1)
    step = advance([heads0], after=(ff1, *down.parts))
    step = advance([heads1], after=step)
    input_grad = input_back(ft0, ft_got, tokens, grad_res, first_gain, after=step)
    step = advance([heads1], after=(input_grad, *heads0.parts))
    (down_sum,) = finish([down], [all_of(0)], [hidden], after=step)
    output = add_output(res, ff0, ff_got, after=(down_sum,))
    mine = wq.shape[1]
    one, two = cut * PAIR, mine - cut * PAIR
    query_sum, key_sum, value_sum, out_sum, norm_sum = finish(
        [heads0, heads1],
        [
            [(i * one, one, (i, 0)) for i in range(3)] + [(3 * one, mine, (3, 0))],
            [(i * two, two, (i, one)) for i in range(3)] + [(3 * two, PAIR, (4, 0))],
        ],
        [mine] * 4 + [PAIR],
        after=(output,),
    )
    return (
        output,
        input_grad,
        query_sum,
        key_sum,
        value_sum,
        out_sum.T,
        gate_sum,
        up_sum,
        down_sum.T,
        norm_sum[:, :4].T,
    )


def solution(mesh):
    in_specs = (
        P(("dp", "tensor"), None),
        P(("dp", "tensor"), None),
        P("dp"),
        P(None, "tensor"),
        P(None, "tensor"),
        P(None, "tensor"),
        P("tensor", None),
        P(),
        P(),
        P(),
        P(),
        P(None, "tensor"),
        P(None, "tensor"),
        P("tensor", None),
    )
    out_specs = (
        P(("dp", "tensor"), None),
        P(("dp", "tensor"), None),
        P("dp", "tensor"),
        P("dp", "tensor"),
        P("dp", "tensor"),
        P("tensor", "dp"),
        P("dp", "tensor"),
        P("dp", "tensor"),
        P("tensor", "dp"),
        P(None, "dp"),
    )
    return jax.shard_map(
        functools.partial(body, mesh.shape["dp"]),
        mesh=mesh,
        in_specs=in_specs,
        out_specs=out_specs,
        check_vma=False,
    )
```

```python
import functools
import math

import jax
import jax.numpy as jnp
from jax import lax
from jax.experimental import pallas as pl
from jax.experimental.pallas import tpu as pltpu
from jax.sharding import PartitionSpec as P

HEAD_DIM = 64
PAIR = 2 * HEAD_DIM
EPS = 1e-05
BASE = 10000.0
BF = jnp.bfloat16
F32 = jnp.float32
SOME = 24 * 1024 * 1024
MOST = 60 * 1024 * 1024
COST = 2

NN = (((1,), (0,)), ((), ()))
NT = (((1,), (1,)), ((), ()))


def dot(left, right, dims=NN):
    return lax.dot_general(left, right, dims, preferred_element_type=F32)


def shape(dims, kind):
    return jax.ShapeDtypeStruct(dims, kind)


def call(
    kernel,
    grid,
    in_specs,
    out_specs,
    out_shape,
    scratch=(),
    flops=0,
    name=None,
    after=(),
    scalars=0,
    limit=SOME,
):
    count = len(after)
    moved = sum(math.prod(s.shape) * s.dtype.itemsize for s in out_shape)

    def ordered(*refs):
        given = scalars + len(in_specs)
        kernel(*refs[:given], *refs[given + count :])

    made = pl.pallas_call(
        ordered,
        grid_spec=pltpu.PrefetchScalarGridSpec(
            num_scalar_prefetch=scalars,
            grid=grid,
            in_specs=list(in_specs) + [pl.BlockSpec(memory_space=pl.ANY)] * count,
            out_specs=out_specs,
            scratch_shapes=scratch,
        ),
        out_shape=out_shape,
        compiler_params=pltpu.CompilerParams(vmem_limit_bytes=limit),
        cost_estimate=pl.CostEstimate(
            flops=int(flops + 3e9) * COST, bytes_accessed=2 * moved, transcendentals=0
        ),
        name=name,
    )
    return lambda *given: made(*given, *after)


SMEM = pl.BlockSpec(memory_space=pltpu.SMEM)


def whole(*dims):
    return pl.BlockSpec(dims, lambda *at: (0,) * len(dims))


def normalize(rows):
    center = rows - jnp.mean(rows, axis=-1, keepdims=True)
    invert = lax.rsqrt(jnp.mean(center * center, axis=-1, keepdims=True) + EPS)
    return center * invert, invert


def norm_back(grad, shaped, invert, gain):
    inner = grad * gain
    return invert * (
        inner
        - jnp.mean(inner, axis=-1, keepdims=True)
        - shaped * jnp.mean(inner * shaped, axis=-1, keepdims=True)
    )


def lower_half(width):
    lane = lax.broadcasted_iota(jnp.int32, (1, width), 1)
    return (lane % HEAD_DIM) < HEAD_DIM // 2


def swap_halves(values):
    width = values.shape[-1]
    half = HEAD_DIM // 2
    return jnp.where(
        lower_half(width), pltpu.roll(values, width - half, 1), pltpu.roll(values, half, 1)
    )


def rotate(values, cosine, sine):
    turned = swap_halves(values)
    return values * cosine + jnp.where(lower_half(values.shape[-1]), -turned, turned) * sine


def unrotate(grad, cosine, sine):
    turned = swap_halves(grad * sine)
    return grad * cosine + jnp.where(lower_half(grad.shape[-1]), turned, -turned)


def rotary_tables(start, length):
    half = HEAD_DIM // 2
    freq = BASE ** (-(jnp.arange(half, dtype=F32) * 2.0 / HEAD_DIM))
    place = (start + jnp.arange(length, dtype=jnp.int32)).astype(F32)
    angle = place[:, None] * jnp.concatenate([freq] * (PAIR // half))[None, :]
    return jnp.cos(angle), jnp.sin(angle)


def project_kernel(scale, x, gain, bias, wq, wk, wv, cos, sin, first_out, q_out, k_out, v_out):
    shaped, _ = normalize(x[...].astype(F32))
    first = (shaped * gain[...] + bias[...]).astype(BF)
    first_out[...] = first
    cosine, sine = cos[...], sin[...]
    for weight, out, factor in ((wq, q_out, scale), (wk, k_out, 1.0)):
        made = dot(first, weight[...])
        for at in range(0, made.shape[1], PAIR):
            turned = rotate(made[:, at : at + PAIR], cosine, sine).astype(BF)
            out[:, at : at + PAIR] = turned * factor if factor != 1.0 else turned
    v_out[...] = dot(first, wv[...]).astype(BF)


def project(x, gain, bias, wq, wk, wv, tables, after=()):
    rows, width = x.shape
    mine = wq.shape[1]
    block = math.gcd(rows, 256)
    row = lambda cols: pl.BlockSpec((block, cols), lambda i: (i, 0))
    scale = HEAD_DIM ** (-0.5)
    return call(
        functools.partial(project_kernel, scale),
        (rows // block,),
        [row(width), whole(1, width), whole(1, width)]
        + [whole(width, mine)] * 3
        + [row(PAIR), row(PAIR)],
        [row(width), row(mine), row(mine), row(mine)],
        [shape((rows, width), BF)] + [shape((rows, mine), BF)] * 3,
        flops=6 * rows * width * mine,
        name="project",
        after=after,
    )(x, gain, bias, wq, wk, wv, *tables)


def attend_kernel(block, q, k0, k1, v0, v1, out, lse):
    lane = lax.broadcasted_iota(jnp.int32, (1, PAIR), 1)
    keys = jnp.concatenate([k0[...], k1[...]], axis=0)
    length = keys.shape[0]
    ones = jnp.where(lax.broadcasted_iota(jnp.int32, (length, PAIR), 1) == 0, 1.0, 0.0).astype(BF)
    values = jnp.concatenate([jnp.concatenate([v0[...], v1[...]], axis=0), ones], axis=1)
    for at in range(0, q.shape[0], block):
        rows = q[at : at + block, :]
        mixed = []
        for head in range(2):
            own = jnp.where((lane // HEAD_DIM) == head, rows, jnp.zeros_like(rows))
            scores = dot(own, keys, NT)
            top = jnp.max(scores, axis=-1, keepdims=True)
            probs = jnp.exp(scores - top).astype(BF)
            summed = dot(probs, values)
            total = summed[:, PAIR : PAIR + 1]
            mixed.append(summed[:, :PAIR] / total)
            lse[0, head, at : at + block] = (top + jnp.log(total))[:, 0]
        out[at : at + block, :] = jnp.where(lane < HEAD_DIM, mixed[0], mixed[1]).astype(BF)


def attend(q, k0, k1, v0, v1, after=()):
    rows, mine = q.shape
    pairs = mine // PAIR
    column = pl.BlockSpec((rows, PAIR), lambda i: (0, i))
    return call(
        functools.partial(attend_kernel, math.gcd(rows, 128)),
        (pairs,),
        [column] * 5,
        [column, pl.BlockSpec((1, 2, rows), lambda i: (i, 0, 0))],
        [shape((rows, mine), BF), shape((pairs, 2, rows), F32)],
        flops=16 * rows * rows * mine,
        name="attend",
        after=after,
    )(q, k0, k1, v0, v1)


def attend_back_kernel(block, *refs):
    (q, k, v, g, o, lse, cos, sin), outs = (
        [refs[2 * i : 2 * i + 2] for i in range(8)],
        refs[16:22],
    )
    dq, dk, dv = outs[0:2], outs[2:4], outs[4:6]
    key_acc, value_acc = refs[22:24]
    lane = lax.broadcasted_iota(jnp.int32, (1, PAIR), 1)
    keys = jnp.concatenate([k[0][...], k[1][...]], axis=0)
    values = jnp.concatenate([v[0][...], v[1][...]], axis=0)
    keys_t = keys.T
    rows = q[0].shape[0]
    scale = HEAD_DIM ** (-0.5)
    started = False
    for part in range(2):
        for at in range(0, rows, block):
            span = slice(at, at + block)
            query, grad = q[part][span, :], g[part][span, :]
            weighed = (grad.astype(F32) * o[part][span, :].astype(F32)).T
            key_sum, value_sum, query_back = None, None, []
            for head in range(2):
                mine = (lane // HEAD_DIM) == head
                own = jnp.where(mine, query, jnp.zeros_like(query))
                own_grad = jnp.where(mine, grad, jnp.zeros_like(grad))
                head_rows = slice(head * HEAD_DIM, (head + 1) * HEAD_DIM)
                delta = jnp.sum(weighed[head_rows, :], axis=0, keepdims=True)
                probs = jnp.exp(dot(keys, own, NT) - lse[part][0, head : head + 1, span])
                grad_scores = (probs * (dot(values, own_grad, NT) - delta)).astype(BF)
                value_one = dot(probs.astype(BF), own_grad)
                key_one = dot(grad_scores, own)
                query_back.append(dot(keys_t[head_rows, :], grad_scores))
                key_sum = key_one if key_sum is None else key_sum + key_one
                value_sum = value_one if value_sum is None else value_sum + value_one
            if started:
                key_acc[...] += key_sum
                value_acc[...] += value_sum
            else:
                key_acc[...] = key_sum
                value_acc[...] = value_sum
                started = True
            back = jnp.concatenate(query_back, axis=0).T * scale
            dq[part][span, :] = unrotate(back, cos[part][span, :], sin[part][span, :]).astype(BF)
    for part in range(2):
        span = slice(part * rows, (part + 1) * rows)
        dk[part][...] = unrotate(key_acc[span, :], cos[part][...], sin[part][...]).astype(BF)
        dv[part][...] = value_acc[span, :].astype(BF)


def attend_back(start, stop, q, k, v, g, o, lse, cos, sin, after=()):
    rows = q[0].shape[0]
    pairs = stop - start
    mine = pairs * PAIR
    column = pl.BlockSpec((rows, PAIR), lambda i: (0, start + i))
    made = pl.BlockSpec((rows, PAIR), lambda i: (0, i))
    stat = pl.BlockSpec((1, 2, rows), lambda i: (start + i, 0, 0))
    table = whole(rows, PAIR)
    outs = call(
        functools.partial(attend_back_kernel, math.gcd(rows, 256)),
        (pairs,),
        [column] * 10 + [stat] * 2 + [table] * 4,
        [made] * 6,
        [shape((rows, mine), BF)] * 6,
        scratch=[pltpu.VMEM((2 * rows, PAIR), F32)] * 2,
        flops=80 * rows * rows * mine,
        name="attend_back",
        after=after,
    )(*q, *k, *v, *g, *o, *lse, *cos, *sin)
    return outs[0:2], outs[2:4], outs[4:6]


def residual_kernel(x, mixed, weight, other, gain, bias, res_out, second_out, *passed):
    for out in passed:
        out[...] = weight[...]
    res = x[...].astype(F32) + dot(mixed[...], weight[...]) + other[...].astype(F32)
    res_out[...] = res
    shaped, _ = normalize(res)
    second_out[...] = (shaped * gain[...] + bias[...]).astype(BF)


def residual(start, rows, x, mixed, weight, other, gain, bias, more, after=()):
    width = x.shape[1]
    mine = mixed.shape[1]
    block = math.gcd(rows, 256)
    row = lambda cols: pl.BlockSpec((block, cols), lambda i: (start // block + i, 0))
    own = pl.BlockSpec((block, width), lambda i: (i, 0))
    return call(
        residual_kernel,
        (rows // block,),
        [row(width), row(mine), whole(mine, width), own, whole(1, width), whole(1, width)],
        [own, own] + [whole(mine, width)] * more,
        [shape((rows, width), F32), shape((rows, width), BF)]
        + [shape((mine, width), BF)] * more,
        flops=2 * rows * width * mine,
        name="residual",
        after=after,
    )(x, mixed, weight, other, gain, bias)


def product_kernel(left, right, out):
    out[...] = dot(left[...], right[...]).astype(out.dtype)


def product_part(start, rows, left, right, after=()):
    return call(
        product_kernel,
        (1,),
        [pl.BlockSpec((rows, left.shape[1]), lambda i: (start // rows, 0)), whole(*right.shape)],
        [whole(rows, right.shape[1])],
        [shape((rows, right.shape[1]), BF)],
        flops=2 * rows * left.shape[1] * right.shape[1],
        name="product_part",
        after=after,
    )(left, right)[0]


def mark_kernel(out):
    out[...] = jnp.zeros_like(out)


def mark(after):
    return call(
        mark_kernel, (1,), [], [whole(8, 128)], [shape((8, 128), F32)], name="mark", after=after
    )()


def down_product(hid, wd, after=()):
    rows, width = hid.shape[0], wd.shape[1]
    block = math.gcd(width, 512)
    return call(
        product_kernel,
        (width // block,),
        [whole(*hid.shape), pl.BlockSpec((wd.shape[0], block), lambda j: (0, j))],
        [pl.BlockSpec((rows, block), lambda j: (0, j))],
        [shape((rows, width), BF)],
        flops=2 * rows * width * wd.shape[0],
        name="down_product",
        after=after,
    )(hid, wd)[0]


def scale_kernel(species, cot, weight, rows_out, hidden_out):
    @pl.when(pl.program_id(0) == 0)
    def _():
        rows_out[...] = (cot[...].astype(F32) * species[0].astype(F32)).astype(BF)

    hidden_out[...] = dot(rows_out[...], weight[...], NT)


def scale_rows(species, cot, weight, after=()):
    rows, width = cot.shape
    hidden = weight.shape[0]
    block = math.gcd(hidden, 512)
    return call(
        scale_kernel,
        (hidden // block,),
        [SMEM, whole(rows, width), pl.BlockSpec((block, width), lambda j: (j, 0))],
        [whole(rows, width), pl.BlockSpec((rows, block), lambda j: (0, j))],
        [shape((rows, width), BF), shape((rows, hidden), F32)],
        flops=2 * rows * width * hidden,
        name="scale_rows",
        limit=MOST,
        after=after,
    )(species, cot, weight)


def feed_kernel(count, forward, *refs):
    seconds, (grad_hidden, wg, wu), refs = refs[:count], refs[count : count + 3], refs[count + 3 :]
    if forward:
        wd, refs = refs[0], refs[1:]
    hid_out, gb_out, ub_out, refs = *refs[:3], refs[3:]
    outs, accs = refs[: 1 + forward], refs[1 + forward :]
    step = pl.program_id(0)
    rows = jnp.concatenate([one[...] for one in seconds], axis=0)
    gate = dot(rows, wg[...])
    upper = dot(rows, wu[...])
    grad_hidden = grad_hidden[...]
    sigma = 0.5 * jnp.tanh(0.5 * gate) + 0.5
    active = gate * sigma
    hidden = (active * upper).astype(BF)
    gate_back = (grad_hidden * upper * (sigma + active * (1.0 - sigma))).astype(BF)
    up_back = (grad_hidden * active).astype(BF)
    hid_out[...] = hidden
    gb_out[...] = gate_back
    ub_out[...] = up_back
    terms = [dot(gate_back, wg[...], NT) + dot(up_back, wu[...], NT)]
    if forward:
        terms.append(dot(hidden, wd[...]))

    @pl.when(step == 0)
    def _():
        for acc, term in zip(accs, terms):
            acc[...] = term

    @pl.when(step > 0)
    def _():
        for acc, term in zip(accs, terms):
            acc[...] += term

    @pl.when(step == pl.num_programs(0) - 1)
    def _():
        for out, acc in zip(outs, accs):
            out[...] = acc[...].astype(out.dtype)


def feed(seconds, grad_hidden, wg, wu, kind, wd=None, after=()):
    rows = sum(one.shape[0] for one in seconds)
    width, hidden = wg.shape
    block = math.gcd(hidden, 512)
    column = pl.BlockSpec((width, block), lambda j: (0, j))
    wide = pl.BlockSpec((rows, block), lambda j: (0, j))
    forward = wd is not None
    more = [wd] if forward else []
    return call(
        functools.partial(feed_kernel, len(seconds), int(forward)),
        (hidden // block,),
        [whole(*one.shape) for one in seconds]
        + [wide, column, column]
        + [pl.BlockSpec((block, width), lambda j: (j, 0))] * forward,
        [wide, wide, wide] + [whole(rows, width)] * (1 + forward),
        [shape((rows, hidden), BF)] * 3 + [shape((rows, width), kind)] * (1 + forward),
        scratch=[pltpu.VMEM((rows, width), F32)] * (1 + forward),
        flops=12 * rows * width * hidden,
        name="feed",
        limit=MOST,
        after=after,
    )(*seconds, grad_hidden, wg, wu, *more)


def flip(out, parts):
    at = 0
    for part in parts:
        rows = part.shape[0]
        out[:, at : at + rows] = part[...].T
        at += rows


def give_out(own, keep, send, span, value):
    value = value.reshape(keep.shape[0], 2, keep.shape[1], value.shape[1])
    even, odd = value[:, 0], value[:, 1]
    keep[:, :, span] = jnp.where(own == 1, odd, even).astype(BF)
    send[:, :, span] = jnp.where(own == 1, even, odd).astype(BF)


def weight_grad_kernel(jobs, core, *refs):
    outs, flipped = refs[-1 - 2 * len(jobs) : -1], refs[-1]
    step = pl.program_id(0)
    at = 0
    for keep, send, (count, pieces, steps, fresh) in zip(outs[::2], outs[1::2], jobs):
        left, refs = refs[:count], refs[count:]
        right, refs = refs[:pieces], refs[pieces:]
        rows = sum(one.shape[0] for one in left)

        if fresh:

            @pl.when(step == at)
            def _():
                flip(flipped, left)

        @pl.when((step >= at) & (step < at + steps))
        def _():
            value = dot(flipped[:, :rows], jnp.concatenate([one[...] for one in right], axis=0))
            give_out(core[0], keep, send, slice(None), value)

        at += steps


def weight_grad(core, parts, jobs, after=()):
    width = jobs[0][0][0].shape[1]
    each = width // parts
    kinds, specs, given, outs, kept, at, most, last_left = [], [], [], [], [], 0, 0, None
    for left, right in jobs:
        wide = right[0].shape[1]
        block = math.gcd(wide, 1024)
        steps = wide // block
        most = max(most, sum(one.shape[0] for one in left))
        column = lambda j, at=at, last=steps - 1: jnp.clip(j - at, 0, last)
        specs += [whole(*one.shape) for one in left]
        specs += [
            pl.BlockSpec((one.shape[0], block), lambda j, column=column: (0, column(j)))
            for one in right
        ]
        given += [*left, *right]
        outs += [
            pl.BlockSpec((parts // 2, each, block), lambda j, column=column: (0, 0, column(j)))
        ] * 2
        kept += [shape((parts // 2, each, wide), BF)] * 2
        kinds.append((len(left), len(right), steps, left is not last_left))
        last_left = left
        at += steps
    return call(
        functools.partial(weight_grad_kernel, kinds),
        (at,),
        [SMEM] + specs,
        outs,
        kept,
        scratch=[pltpu.VMEM((width, most), BF)],
        flops=2 * most * width * sum(job[1][0].shape[1] for job in jobs),
        name="weight_grad",
        limit=MOST,
        after=after,
    )(core, *given)


def head_grad_kernel(count, with_out, core, *refs):
    first, backs, refs = refs[:2], refs[2 : 2 + 2 * count], refs[2 + 2 * count :]
    keep, send, flipped = refs[-3:]
    flip(flipped, first)
    at = 0
    for i in range(count):
        right = jnp.concatenate([backs[2 * i][...], backs[2 * i + 1][...]], axis=0)
        wide = right.shape[1]
        give_out(core[0], keep, send, slice(at, at + wide), dot(flipped[...], right))
        at += wide
    if with_out:
        flip(flipped, refs[0:2])
        right = jnp.concatenate([refs[2][...], refs[3][...]], axis=0)
        give_out(core[0], keep, send, slice(at, at + right.shape[1]), dot(flipped[...], right))
    else:
        rows = [refs[0][...]]
        rows.append(jnp.zeros((PAIR - 4, rows[0].shape[1]), F32))
        value = jnp.concatenate(rows, axis=0).T
        give_out(core[0], keep, send, slice(at, at + PAIR), value)


def head_grad(core, parts, first, backs, out_job=(), terms=(), after=()):
    rows, width = first[0].shape
    each = width // parts
    total = sum(back[0].shape[1] for back in backs)
    total += out_job[2].shape[1] if out_job else PAIR
    given = [*first, *[half for pair in backs for half in pair], *out_job, *terms]
    out = whole(parts // 2, each, total)
    return call(
        functools.partial(head_grad_kernel, len(backs), bool(out_job)),
        (1,),
        [SMEM] + [whole(*one.shape) for one in given],
        [out] * 2,
        [shape((parts // 2, each, total), BF)] * 2,
        scratch=[pltpu.VMEM((width, 2 * rows), BF)],
        flops=4 * rows * width * total,
        name="head_grad",
        after=after,
    )(core, *given)


def res_back_kernel(
    species, own, other, cot, res0, res1, gain, w0, w1, *outs
):
    grad_out, attn_out, gm0_out, gm1_out, terms_out = outs
    res = jnp.where(pl.program_id(0) == 0, res0[...], res1[...])
    grad = own[...] + other[...].astype(F32)
    shaped, invert = normalize(res)
    made = cot[...].astype(F32) * species[0].astype(F32) + norm_back(
        grad, shaped, invert, gain[...]
    )
    grad_out[...] = made
    attn = made.astype(BF)
    attn_out[...] = attn
    gm1_out[...] = dot(attn, w1[...], NT).astype(BF)
    gm0_out[...] = dot(attn, w0[...], NT).astype(BF)

    @pl.when(pl.program_id(0) == 0)
    def _():
        terms_out[...] = jnp.zeros_like(terms_out)

    terms_out[0:1, :] += jnp.sum(grad * shaped, axis=0, keepdims=True)
    terms_out[1:2, :] += jnp.sum(grad, axis=0, keepdims=True)


def res_back(species, own, other, cot, res, gain, w0, w1, after=()):
    rows, width = own.shape
    mine = w0.shape[0]
    block = rows // 2
    row = lambda cols: pl.BlockSpec((block, cols), lambda i: (i, 0))
    return call(
        res_back_kernel,
        (rows // block,),
        [SMEM] + [row(width)] * 3 + [whole(block, width)] * 2
        + [whole(1, width)] + [whole(mine, width)] * 2,
        [row(width), row(width), row(mine), row(mine), whole(2, width)],
        [
            shape((rows, width), F32),
            shape((rows, width), BF),
            shape((rows, mine), BF),
            shape((rows, mine), BF),
            shape((2, width), F32),
        ],
        flops=4 * rows * width * mine,
        name="res_back",
        limit=MOST,
        after=after,
    )(species, own, other, cot, *res, gain, w0, w1)


def first_back_kernel(count, half, *refs):
    sides, refs = (refs[: 3 * count], refs[3 * count : 6 * count]), refs[6 * count :]
    weights, tokens, (more, out1, out0, terms_out) = refs[:3], refs[3:5], refs[5:]

    @pl.when(pl.program_id(0) == 0)
    def _():
        terms_out[0:2, :] = jnp.zeros_like(more)
        terms_out[2:4, :] = more[...]

    for side, (backs, x, out) in enumerate(zip(sides, tokens, (out1, out0))):

        @pl.when(within(pl.program_id(0), side * half, half))
        def _():
            grad = None
            for i in range(3):
                beside = [one[...] for one in backs[i * count : (i + 1) * count]]
                term = dot(jnp.concatenate(beside, axis=1), weights[i][...], NT)
                grad = term if grad is None else grad + term
            out[...] = grad.astype(out.dtype)
            shaped, _ = normalize(x[...].astype(F32))
            terms_out[0:1, :] += jnp.sum(grad * shaped, axis=0, keepdims=True)
            terms_out[1:2, :] += jnp.sum(grad, axis=0, keepdims=True)


def first_back(groups, wq, wk, wv, tokens, terms, after=()):
    rows, width = tokens[0].shape
    mine = wq.shape[1]
    count = len(groups)
    block = math.gcd(rows, 256)
    half = rows // block
    given, specs = [], []
    for side in (1, 0):
        at = half * (1 - side)
        place = lambda i, at=at: (jnp.clip(i - at, 0, half - 1), 0)
        for kind in range(3):
            for group in groups:
                given.append(group[kind][side])
                specs.append(pl.BlockSpec((block, given[-1].shape[1]), place))
    outs = [
        pl.BlockSpec((block, width), lambda i, at=at: (jnp.clip(i - at, 0, half - 1), 0))
        for at in (0, half)
    ]
    return call(
        functools.partial(first_back_kernel, count, half),
        (2 * half,),
        specs + [whole(width, mine)] * 3 + outs + [whole(2, width)],
        outs + [whole(4, width)],
        [shape((rows, width), BF), shape((rows, width), F32), shape((4, width), F32)],
        flops=12 * rows * width * mine,
        name="first_back",
        after=after,
    )(*given, wq, wk, wv, tokens[1], tokens[0], terms)


def input_back_kernel(own, other, x, res, gain, out):
    shaped, invert = normalize(x[...].astype(F32))
    grad = own[...] + other[...].astype(F32)
    out[...] = res[...] + norm_back(grad, shaped, invert, gain[...])


def input_back(own, other, x, res, gain, after=()):
    rows, width = x.shape
    block = math.gcd(rows, 128)
    row = pl.BlockSpec((block, width), lambda i: (i, 0))
    return call(
        input_back_kernel,
        (rows // block,),
        [row] * 4 + [whole(1, width)],
        [row],
        [shape((rows, width), F32)],
        name="input_back",
        limit=MOST,
        after=after,
    )(own, other, x, res, gain)[0]


def output_kernel(res0, res1, own, other, out):
    res = jnp.where(pl.program_id(0) == 0, res0[...], res1[...])
    out[...] = (res + own[...] + other[...].astype(F32)).astype(out.dtype)


def add_output(res, own, other, after=()):
    rows, width = own.shape
    block = rows // 2
    row = pl.BlockSpec((block, width), lambda i: (i, 0))
    return call(
        output_kernel,
        (2,),
        [whole(block, width)] * 2 + [row] * 2,
        [row],
        [shape((rows, width), BF)],
        name="add_output",
        after=after,
    )(*res, own, other)[0]


def pair_swap(values):
    return lax.ppermute(values, "tensor", [(0, 1), (1, 0)])


def dp_swap(values, turn, parts):
    return lax.ppermute(values, "dp", [(i, i ^ turn) for i in range(parts)])


def within(step, start, steps):
    return (step >= start) & (step < start + steps)


def total_of(refs):
    total = refs[0][...].astype(F32)
    for one in refs[1:]:
        total = total + one[...].astype(F32)
    return total


def combine_kernel(spans, places, *refs):
    count = sum(terms * shares for _, _, terms, shares in spans)
    ins, outs = refs[:count], refs[count:]
    for start, steps, terms, shares in spans:
        given, ins = ins[: terms * shares], ins[terms * shares :]
        made, outs = outs[:shares], outs[shares:]

        @pl.when(within(pl.program_id(0), start, steps))
        def _():
            for r in range(shares):
                made[r][...] = total_of(given[r * terms : (r + 1) * terms]).astype(BF)


class Scatter:
    def __init__(self, keep, send, order, count, place):
        self.count, self.place, self.order = count, place, list(order)
        self.left = list(range(count.bit_length() - 2, 0, -1))
        self.parts = [keep, dp_swap(send, 1, count)]


def advance(chains, after=()):
    chains = [chain for chain in chains if chain.order]
    if not chains:
        return tuple(after)
    spans, places, given, ins, outs, shapes, begin = [], [], [], [], [], [], 0
    for i, chain in enumerate(chains):
        bits = chain.order.pop(0)
        shares = 2 ** len(bits)
        axis = chain.left.index(bits[-1])
        for bit in bits:
            chain.left.remove(bit)
        each, columns = chain.parts[0].shape[-2:]
        high, low = 2**axis, 2 ** (len(chain.left) - axis)
        view = (high, shares, low, each, columns)
        block = 1024 if columns % 1024 == 0 else columns
        last = columns // block - 1
        block_of = lambda j, begin=begin, last=last: jnp.clip(j - begin, 0, last)
        for r in range(shares):
            share = pl.BlockSpec(
                (high, None, low, each, block),
                lambda j, at, i=i, r=r, block_of=block_of: (0, at[i] ^ r, 0, 0, block_of(j)),
            )
            ins += [share] * len(chain.parts)
            given += [one.reshape(view) for one in chain.parts]
        out = pl.BlockSpec(
            (high, low, each, block), lambda j, at, block_of=block_of: (0, 0, 0, block_of(j))
        )
        outs += [out] * shares
        shapes += [shape((high, low, each, columns), BF)] * shares
        spans.append((begin, last + 1, len(chain.parts), shares))
        places.append((chain.place >> bits[0]) & (shares - 1))
        chain.bits, chain.shares = bits, shares
        begin += last + 1
    made = call(
        functools.partial(combine_kernel, spans),
        (begin,),
        ins,
        outs,
        shapes,
        name="combine",
        after=after,
        scalars=1,
    )(jnp.stack(places).astype(jnp.int32), *given)
    first = made[0]
    for chain in chains:
        own, made = made[: chain.shares], made[chain.shares :]
        chain.parts = [own[0]] + [
            dp_swap(own[r], r << chain.bits[0], chain.count) for r in range(1, chain.shares)
        ]
    return (first,)


def finish_kernel(counts, cuts, *refs):
    total = sum(counts)
    ins, outs = refs[:total], refs[total:]
    for count, cut in zip(counts, cuts):
        given, ins = ins[:count], ins[count:]
        value = total_of(given)
        for at, wide, to in cut:
            out, low = outs[to[0]], to[1]
            out[:, low : low + wide] = value[:, at : at + wide]


def finish(chains, cuts, columns, after=()):
    while any(chain.order for chain in chains):
        after = advance(chains, after)
    given, counts = [], []
    for chain in chains:
        flat = chain.parts[0].shape[-2:]
        counts.append(len(chain.parts))
        given += [one.reshape(flat) for one in chain.parts]
    rows = given[0].shape[0]
    return call(
        functools.partial(finish_kernel, counts, cuts),
        (1,),
        [whole(*one.shape) for one in given],
        [whole(rows, wide) for wide in columns],
        [shape((rows, wide), F32) for wide in columns],
        name="finish",
        limit=MOST,
        after=after,
    )(*given)


def body(
    parts,
    tokens,
    cotangent,
    species,
    wq,
    wk,
    wv,
    wo,
    first_gain,
    first_bias,
    second_gain,
    second_bias,
    wg,
    wu,
    wd,
):
    place = lax.axis_index("dp")
    half = lax.axis_index("tensor")
    core = (place & 1).astype(jnp.int32).reshape(1)
    rows = tokens.shape[0]
    bits = parts.bit_length() - 1
    wide = [[bit] for bit in range(2, bits)]
    low_first = [[1]] * (bits > 1) + wide
    high_first = wide + [[1]] * (bits > 1)
    first_gain, first_bias = first_gain[None], first_bias[None]
    second_gain, second_bias = second_gain[None], second_bias[None]

    tokens1 = pair_swap(tokens)
    cot1 = pair_swap(cotangent)
    table0 = rotary_tables(half * rows, rows)
    table1 = rotary_tables((1 - half) * rows, rows)
    first0, q0, k0, v0 = project(tokens, first_gain, first_bias, wq, wk, wv, table0)
    gr0, grad_hidden0 = scale_rows(species, cotangent, wd, after=(first0,))
    first1, q1, k1, v1 = project(
        tokens1, first_gain, first_bias, wq, wk, wv, table1, after=(gr0,)
    )
    mixed1, lse1 = attend(q1, k0, k1, v0, v1)
    cut = rows // 2
    attn_a = product_part(0, cut, mixed1, wo)
    attn_b = product_part(cut, rows - cut, mixed1, wo, after=(attn_a,))
    got_a, got_b = pair_swap(attn_a), pair_swap(attn_b)
    mixed0, lse0 = attend(q0, k0, k1, v0, v1, after=(attn_b,))
    gr1, grad_hidden1 = scale_rows(species, cot1, wd, after=(mixed0,))
    second = lambda start, got, more, after: residual(
        start, cut, tokens, mixed0, wo, got, second_gain, second_bias, more, after=after
    )
    res_a, second0a = second(0, got_a, 0, (grad_hidden1,))
    res_b, second0b, wo_late = second(cut, got_b, 1, (res_a,))
    res = (res_a, res_b)
    second1a, second1b = pair_swap(second0a), pair_swap(second0b)
    wo1 = pair_swap(wo_late)
    hid0, gb0, ub0, st0, ff0 = feed((second0a, second0b), grad_hidden0, wg, wu, F32, wd)
    hid1, gb1, ub1, st1 = feed((second1a, second1b), grad_hidden1, wg, wu, BF, after=mark((st0, second1a)))

    st_got = pair_swap(st1)
    seconds = [second0a, second0b, second1a, second1b]
    gate_keep, gate_send, up_keep, up_send = weight_grad(
        core, parts, [(seconds, [gb0, gb1]), (seconds, [ub0, ub1])], after=(st1,)
    )
    gate = Scatter(gate_keep, gate_send, low_first, parts, place)
    up = Scatter(up_keep, up_send, high_first, parts, place)
    down_keep, down_send = weight_grad(
        core, parts, [([gr0, gr1], [hid0, hid1])], after=(gate_keep, wo1)
    )
    down = Scatter(down_keep, down_send, low_first, parts, place)
    grad_res, attn_grad0, gm0, gm_give, second_terms = res_back(
        species, st0, st_got, cotangent, res, second_gain, wo, wo1, after=(down_keep,)
    )
    gm1 = pair_swap(gm_give)
    attn_grad1 = pair_swap(attn_grad0)
    step = advance([gate], after=(grad_res,))
    step = advance([up], after=step)
    step = advance([down], after=step)

    pairs = q0.shape[1] // PAIR
    back = lambda start, stop, after: attend_back(
        start,
        stop,
        (q0, q1),
        (k0, k1),
        (v0, v1),
        (gm0, gm1),
        (mixed0, mixed1),
        (lse0, lse1),
        (table0[0], table1[0]),
        (table0[1], table1[1]),
        after=after,
    )
    cut = pairs // 2
    firsts = (first0, first1)
    low = back(0, cut, step)
    ff1 = down_product(hid1, wd, after=(low[0][0],))
    ff_got = pair_swap(ff1)
    step = advance([gate], after=(ff1,))
    step = advance([up], after=step)
    low_keep, low_send = head_grad(
        core, parts, firsts, low, out_job=(attn_grad0, attn_grad1, mixed0, mixed1), after=step
    )
    heads0 = Scatter(low_keep, low_send, low_first, parts, place)
    high = back(cut, pairs, (low_keep,))
    step = advance([down], after=(high[0][0],))
    step = advance([gate], after=step)
    step = advance([up], after=step)
    step = advance([heads0], after=step)
    ft1, ft0, terms = first_back(
        (low, high), wq, wk, wv, (tokens, tokens1), second_terms, after=step
    )
    ft_got = pair_swap(ft1)
    high_keep, high_send = head_grad(core, parts, firsts, high, terms=(terms,), after=(ft1,))
    heads1 = Scatter(high_keep, high_send, low_first, parts, place)
    output = add_output(res, ff0, ff_got, after=(high_keep,))
    step = advance([down], after=mark((output, *gate.parts, *up.parts)))
    step = advance([heads0], after=step)
    step = advance([heads1], after=step)
    step = advance([heads0], after=mark((*step, *down.parts)))
    step = advance([heads1], after=step)
    step = advance([heads1], after=step)
    input_grad = input_back(ft0, ft_got, tokens, grad_res, first_gain, after=step)
    step = (input_grad,)
    hidden = wg.shape[1]
    mine = wq.shape[1]
    one, two = cut * PAIR, mine - cut * PAIR
    all_of = lambda to: [(0, hidden, (to, 0))]
    query_sum, key_sum, value_sum, out_sum, norm_sum = finish(
        [heads0, heads1],
        [
            [(i * one, one, (i, 0)) for i in range(3)] + [(3 * one, mine, (3, 0))],
            [(i * two, two, (i, one)) for i in range(3)] + [(3 * two, PAIR, (4, 0))],
        ],
        [mine] * 4 + [PAIR],
        after=step,
    )
    gate_sum, up_sum, down_sum = finish(
        [gate, up, down], [all_of(i) for i in range(3)], [hidden] * 3, after=(query_sum,)
    )
    norm_sum = norm_sum[:, :4]
    norm_sum = norm_sum + pair_swap(norm_sum)
    return (
        output,
        input_grad,
        query_sum,
        key_sum,
        value_sum,
        out_sum.T,
        gate_sum,
        up_sum,
        down_sum.T,
        norm_sum.T,
    )


def solution(mesh):
    in_specs = (
        P(("dp", "tensor"), None),
        P(("dp", "tensor"), None),
        P("dp"),
        P(None, "tensor"),
        P(None, "tensor"),
        P(None, "tensor"),
        P("tensor", None),
        P(),
        P(),
        P(),
        P(),
        P(None, "tensor"),
        P(None, "tensor"),
        P("tensor", None),
    )
    out_specs = (
        P(("dp", "tensor"), None),
        P(("dp", "tensor"), None),
        P("dp", "tensor"),
        P("dp", "tensor"),
        P("dp", "tensor"),
        P("tensor", "dp"),
        P("dp", "tensor"),
        P("dp", "tensor"),
        P("tensor", "dp"),
        P(None, "dp"),
    )
    return jax.shard_map(
        functools.partial(body, mesh.shape["dp"]),
        mesh=mesh,
        in_specs=in_specs,
        out_specs=out_specs,
        check_vma=False,
    )
```

```python
import functools
import math

import jax
import jax.numpy as jnp
from jax import lax
from jax.experimental import pallas as pl
from jax.experimental.pallas import tpu as pltpu
from jax.sharding import PartitionSpec as P

HEAD_DIM = 64
PAIR = 2 * HEAD_DIM
EPS = 1e-05
BASE = 10000.0
BF = jnp.bfloat16
F32 = jnp.float32
SOME = 24 * 1024 * 1024
MOST = 60 * 1024 * 1024
RATE = 3e9
LENGTH = {
    "project": 3.6,
    "scale_rows": 6.8,
    "attend": 7.2,
    "product_part": 1.0,
    "residual": 2.8,
    "mark": 0.4,
    "feed": 17.0,
    "weight_grad": 13.0,
    "res_back": 7.6,
    "combine": 1.0,
    "attend_back": 11.7,
    "down_product": 2.8,
    "head_grad": 2.4,
    "first_back": 6.0,
    "add_output": 1.3,
    "input_back": 5.3,
    "finish": 2.2,
}

NN = (((1,), (0,)), ((), ()))
NT = (((1,), (1,)), ((), ()))


def dot(left, right, dims=NN):
    return lax.dot_general(left, right, dims, preferred_element_type=F32)


def shape(dims, kind):
    return jax.ShapeDtypeStruct(dims, kind)


def call(
    kernel,
    grid,
    in_specs,
    out_specs,
    out_shape,
    scratch=(),
    flops=0,
    name=None,
    after=(),
    scalars=0,
    limit=SOME,
):
    count = len(after)
    moved = sum(math.prod(s.shape) * s.dtype.itemsize for s in out_shape)

    def ordered(*refs):
        given = scalars + len(in_specs)
        kernel(*refs[:given], *refs[given + count :])

    made = pl.pallas_call(
        ordered,
        grid_spec=pltpu.PrefetchScalarGridSpec(
            num_scalar_prefetch=scalars,
            grid=grid,
            in_specs=list(in_specs) + [pl.BlockSpec(memory_space=pl.ANY)] * count,
            out_specs=out_specs,
            scratch_shapes=scratch,
        ),
        out_shape=out_shape,
        compiler_params=pltpu.CompilerParams(vmem_limit_bytes=limit),
        cost_estimate=pl.CostEstimate(
            flops=int(LENGTH[name] * RATE), bytes_accessed=2 * moved, transcendentals=0
        ),
        name=name,
    )
    return lambda *given: made(*given, *after)


SMEM = pl.BlockSpec(memory_space=pltpu.SMEM)


def whole(*dims):
    return pl.BlockSpec(dims, lambda *at: (0,) * len(dims))


def normalize(rows):
    center = rows - jnp.mean(rows, axis=-1, keepdims=True)
    invert = lax.rsqrt(jnp.mean(center * center, axis=-1, keepdims=True) + EPS)
    return center * invert, invert


def norm_back(grad, shaped, invert, gain):
    inner = grad * gain
    return invert * (
        inner
        - jnp.mean(inner, axis=-1, keepdims=True)
        - shaped * jnp.mean(inner * shaped, axis=-1, keepdims=True)
    )


def lower_half(width):
    lane = lax.broadcasted_iota(jnp.int32, (1, width), 1)
    return (lane % HEAD_DIM) < HEAD_DIM // 2


def swap_halves(values):
    width = values.shape[-1]
    half = HEAD_DIM // 2
    return jnp.where(
        lower_half(width), pltpu.roll(values, width - half, 1), pltpu.roll(values, half, 1)
    )


def rotate(values, cosine, sine):
    turned = swap_halves(values)
    return values * cosine + jnp.where(lower_half(values.shape[-1]), -turned, turned) * sine


def unrotate(grad, cosine, sine):
    turned = swap_halves(grad * sine)
    return grad * cosine + jnp.where(lower_half(grad.shape[-1]), turned, -turned)


def rotary_tables(start, length):
    half = HEAD_DIM // 2
    freq = BASE ** (-(jnp.arange(half, dtype=F32) * 2.0 / HEAD_DIM))
    place = (start + jnp.arange(length, dtype=jnp.int32)).astype(F32)
    angle = place[:, None] * jnp.concatenate([freq] * (PAIR // half))[None, :]
    return jnp.cos(angle), jnp.sin(angle)


def project_kernel(scale, x, gain, bias, wq, wk, wv, cos, sin, first_out, q_out, k_out, v_out):
    shaped, _ = normalize(x[...].astype(F32))
    first = (shaped * gain[...] + bias[...]).astype(BF)
    first_out[...] = first
    cosine, sine = cos[...], sin[...]
    for weight, out, factor in ((wq, q_out, scale), (wk, k_out, 1.0)):
        made = dot(first, weight[...])
        for at in range(0, made.shape[1], PAIR):
            turned = rotate(made[:, at : at + PAIR], cosine, sine).astype(BF)
            out[:, at : at + PAIR] = turned * factor if factor != 1.0 else turned
    v_out[...] = dot(first, wv[...]).astype(BF)


def project(x, gain, bias, wq, wk, wv, tables, after=()):
    rows, width = x.shape
    mine = wq.shape[1]
    block = math.gcd(rows, 256)
    row = lambda cols: pl.BlockSpec((block, cols), lambda i: (i, 0))
    scale = HEAD_DIM ** (-0.5)
    return call(
        functools.partial(project_kernel, scale),
        (rows // block,),
        [row(width), whole(1, width), whole(1, width)]
        + [whole(width, mine)] * 3
        + [row(PAIR), row(PAIR)],
        [row(width), row(mine), row(mine), row(mine)],
        [shape((rows, width), BF)] + [shape((rows, mine), BF)] * 3,
        flops=6 * rows * width * mine,
        name="project",
        after=after,
    )(x, gain, bias, wq, wk, wv, *tables)


def attend_kernel(block, q, k0, k1, v0, v1, out, lse):
    lane = lax.broadcasted_iota(jnp.int32, (1, PAIR), 1)
    keys = jnp.concatenate([k0[...], k1[...]], axis=0)
    length = keys.shape[0]
    ones = jnp.where(lax.broadcasted_iota(jnp.int32, (length, PAIR), 1) == 0, 1.0, 0.0).astype(BF)
    values = jnp.concatenate([jnp.concatenate([v0[...], v1[...]], axis=0), ones], axis=1)
    for at in range(0, q.shape[0], block):
        rows = q[at : at + block, :]
        mixed = []
        for head in range(2):
            own = jnp.where((lane // HEAD_DIM) == head, rows, jnp.zeros_like(rows))
            scores = dot(own, keys, NT)
            top = jnp.max(scores, axis=-1, keepdims=True)
            probs = jnp.exp(scores - top).astype(BF)
            summed = dot(probs, values)
            total = summed[:, PAIR : PAIR + 1]
            mixed.append(summed[:, :PAIR] / total)
            lse[0, head, at : at + block] = (top + jnp.log(total))[:, 0]
        out[at : at + block, :] = jnp.where(lane < HEAD_DIM, mixed[0], mixed[1]).astype(BF)


def attend(q, k0, k1, v0, v1, after=()):
    rows, mine = q.shape
    pairs = mine // PAIR
    column = pl.BlockSpec((rows, PAIR), lambda i: (0, i))
    return call(
        functools.partial(attend_kernel, math.gcd(rows, 128)),
        (pairs,),
        [column] * 5,
        [column, pl.BlockSpec((1, 2, rows), lambda i: (i, 0, 0))],
        [shape((rows, mine), BF), shape((pairs, 2, rows), F32)],
        flops=16 * rows * rows * mine,
        name="attend",
        after=after,
    )(q, k0, k1, v0, v1)


def attend_back_kernel(block, *refs):
    (q, k, v, g, o, lse, cos, sin), outs = (
        [refs[2 * i : 2 * i + 2] for i in range(8)],
        refs[16:22],
    )
    dq, dk, dv = outs[0:2], outs[2:4], outs[4:6]
    key_acc, value_acc = refs[22:24]
    lane = lax.broadcasted_iota(jnp.int32, (1, PAIR), 1)
    keys = jnp.concatenate([k[0][...], k[1][...]], axis=0)
    values = jnp.concatenate([v[0][...], v[1][...]], axis=0)
    keys_t = keys.T
    rows = q[0].shape[0]
    scale = HEAD_DIM ** (-0.5)
    started = False
    for part in range(2):
        for at in range(0, rows, block):
            span = slice(at, at + block)
            query, grad = q[part][span, :], g[part][span, :]
            weighed = (grad.astype(F32) * o[part][span, :].astype(F32)).T
            key_sum, value_sum, query_back = None, None, []
            for head in range(2):
                mine = (lane // HEAD_DIM) == head
                own = jnp.where(mine, query, jnp.zeros_like(query))
                own_grad = jnp.where(mine, grad, jnp.zeros_like(grad))
                head_rows = slice(head * HEAD_DIM, (head + 1) * HEAD_DIM)
                delta = jnp.sum(weighed[head_rows, :], axis=0, keepdims=True)
                probs = jnp.exp(dot(keys, own, NT) - lse[part][0, head : head + 1, span])
                grad_scores = (probs * (dot(values, own_grad, NT) - delta)).astype(BF)
                value_one = dot(probs.astype(BF), own_grad)
                key_one = dot(grad_scores, own)
                query_back.append(dot(keys_t[head_rows, :], grad_scores))
                key_sum = key_one if key_sum is None else key_sum + key_one
                value_sum = value_one if value_sum is None else value_sum + value_one
            if started:
                key_acc[...] += key_sum
                value_acc[...] += value_sum
            else:
                key_acc[...] = key_sum
                value_acc[...] = value_sum
                started = True
            back = jnp.concatenate(query_back, axis=0).T * scale
            dq[part][span, :] = unrotate(back, cos[part][span, :], sin[part][span, :]).astype(BF)
    for part in range(2):
        span = slice(part * rows, (part + 1) * rows)
        dk[part][...] = unrotate(key_acc[span, :], cos[part][...], sin[part][...]).astype(BF)
        dv[part][...] = value_acc[span, :].astype(BF)


def attend_back(start, stop, q, k, v, g, o, lse, cos, sin, after=()):
    rows = q[0].shape[0]
    pairs = stop - start
    mine = pairs * PAIR
    column = pl.BlockSpec((rows, PAIR), lambda i: (0, start + i))
    made = pl.BlockSpec((rows, PAIR), lambda i: (0, i))
    stat = pl.BlockSpec((1, 2, rows), lambda i: (start + i, 0, 0))
    table = whole(rows, PAIR)
    outs = call(
        functools.partial(attend_back_kernel, math.gcd(rows, 256)),
        (pairs,),
        [column] * 10 + [stat] * 2 + [table] * 4,
        [made] * 6,
        [shape((rows, mine), BF)] * 6,
        scratch=[pltpu.VMEM((2 * rows, PAIR), F32)] * 2,
        flops=80 * rows * rows * mine,
        name="attend_back",
        after=after,
    )(*q, *k, *v, *g, *o, *lse, *cos, *sin)
    return outs[0:2], outs[2:4], outs[4:6]


def residual_kernel(x, mixed, weight, other, gain, bias, res_out, second_out, *passed):
    for out in passed:
        out[...] = weight[...]
    res = x[...].astype(F32) + dot(mixed[...], weight[...]) + other[...].astype(F32)
    res_out[...] = res
    shaped, _ = normalize(res)
    second_out[...] = (shaped * gain[...] + bias[...]).astype(BF)


def residual(start, rows, x, mixed, weight, other, gain, bias, more, after=()):
    width = x.shape[1]
    mine = mixed.shape[1]
    block = math.gcd(rows, 256)
    row = lambda cols: pl.BlockSpec((block, cols), lambda i: (start // block + i, 0))
    own = pl.BlockSpec((block, width), lambda i: (i, 0))
    return call(
        residual_kernel,
        (rows // block,),
        [row(width), row(mine), whole(mine, width), own, whole(1, width), whole(1, width)],
        [own, own] + [whole(mine, width)] * more,
        [shape((rows, width), F32), shape((rows, width), BF)]
        + [shape((mine, width), BF)] * more,
        flops=2 * rows * width * mine,
        name="residual",
        after=after,
    )(x, mixed, weight, other, gain, bias)


def product_kernel(left, right, out):
    out[...] = dot(left[...], right[...]).astype(out.dtype)


def product_part(start, rows, left, right, after=()):
    return call(
        product_kernel,
        (1,),
        [pl.BlockSpec((rows, left.shape[1]), lambda i: (start // rows, 0)), whole(*right.shape)],
        [whole(rows, right.shape[1])],
        [shape((rows, right.shape[1]), BF)],
        flops=2 * rows * left.shape[1] * right.shape[1],
        name="product_part",
        after=after,
    )(left, right)[0]


def mark_kernel(out):
    out[...] = jnp.zeros_like(out)


def mark(after):
    return call(
        mark_kernel, (1,), [], [whole(8, 128)], [shape((8, 128), F32)], name="mark", after=after
    )()


def down_product(hid, wd, after=()):
    rows, width = hid.shape[0], wd.shape[1]
    block = math.gcd(width, 512)
    return call(
        product_kernel,
        (width // block,),
        [whole(*hid.shape), pl.BlockSpec((wd.shape[0], block), lambda j: (0, j))],
        [pl.BlockSpec((rows, block), lambda j: (0, j))],
        [shape((rows, width), BF)],
        flops=2 * rows * width * wd.shape[0],
        name="down_product",
        after=after,
    )(hid, wd)[0]


def scale_kernel(species, cot, weight, rows_out, hidden_out):
    @pl.when(pl.program_id(0) == 0)
    def _():
        rows_out[...] = (cot[...].astype(F32) * species[0].astype(F32)).astype(BF)

    hidden_out[...] = dot(rows_out[...], weight[...], NT)


def scale_rows(species, cot, weight, after=()):
    rows, width = cot.shape
    hidden = weight.shape[0]
    block = math.gcd(hidden, 512)
    return call(
        scale_kernel,
        (hidden // block,),
        [SMEM, whole(rows, width), pl.BlockSpec((block, width), lambda j: (j, 0))],
        [whole(rows, width), pl.BlockSpec((rows, block), lambda j: (0, j))],
        [shape((rows, width), BF), shape((rows, hidden), F32)],
        flops=2 * rows * width * hidden,
        name="scale_rows",
        after=after,
    )(species, cot, weight)


def feed_kernel(count, forward, *refs):
    seconds, (grad_hidden, wg, wu), refs = refs[:count], refs[count : count + 3], refs[count + 3 :]
    if forward:
        wd, refs = refs[0], refs[1:]
    hid_out, gb_out, ub_out, refs = *refs[:3], refs[3:]
    outs, accs = refs[: 1 + forward], refs[1 + forward :]
    step = pl.program_id(0)
    rows = jnp.concatenate([one[...] for one in seconds], axis=0)
    gate = dot(rows, wg[...])
    upper = dot(rows, wu[...])
    grad_hidden = grad_hidden[...]
    sigma = 0.5 * jnp.tanh(0.5 * gate) + 0.5
    active = gate * sigma
    hidden = (active * upper).astype(BF)
    gate_back = (grad_hidden * upper * (sigma + active * (1.0 - sigma))).astype(BF)
    up_back = (grad_hidden * active).astype(BF)
    hid_out[...] = hidden
    gb_out[...] = gate_back
    ub_out[...] = up_back
    terms = [dot(gate_back, wg[...], NT) + dot(up_back, wu[...], NT)]
    if forward:
        terms.append(dot(hidden, wd[...]))

    @pl.when(step == 0)
    def _():
        for acc, term in zip(accs, terms):
            acc[...] = term

    @pl.when(step > 0)
    def _():
        for acc, term in zip(accs, terms):
            acc[...] += term

    @pl.when(step == pl.num_programs(0) - 1)
    def _():
        for out, acc in zip(outs, accs):
            out[...] = acc[...].astype(out.dtype)


def feed(seconds, grad_hidden, wg, wu, kind, wd=None, after=()):
    rows = sum(one.shape[0] for one in seconds)
    width, hidden = wg.shape
    block = math.gcd(hidden, 512)
    column = pl.BlockSpec((width, block), lambda j: (0, j))
    wide = pl.BlockSpec((rows, block), lambda j: (0, j))
    forward = wd is not None
    more = [wd] if forward else []
    return call(
        functools.partial(feed_kernel, len(seconds), int(forward)),
        (hidden // block,),
        [whole(*one.shape) for one in seconds]
        + [wide, column, column]
        + [pl.BlockSpec((block, width), lambda j: (j, 0))] * forward,
        [wide, wide, wide] + [whole(rows, width)] * (1 + forward),
        [shape((rows, hidden), BF)] * 3 + [shape((rows, width), kind)] * (1 + forward),
        scratch=[pltpu.VMEM((rows, width), F32)] * (1 + forward),
        flops=12 * rows * width * hidden,
        name="feed",
        after=after,
    )(*seconds, grad_hidden, wg, wu, *more)


def flip(out, parts):
    at = 0
    for part in parts:
        rows = part.shape[0]
        out[:, at : at + rows] = part[...].T
        at += rows


def give_out(own, keep, send, span, value):
    value = value.reshape(keep.shape[0], 2, keep.shape[1], value.shape[1])
    even, odd = value[:, 0], value[:, 1]
    keep[:, :, span] = jnp.where(own == 1, odd, even).astype(BF)
    send[:, :, span] = jnp.where(own == 1, even, odd).astype(BF)


def weight_grad_kernel(jobs, core, *refs):
    outs, flipped = refs[-1 - 2 * len(jobs) : -1], refs[-1]
    step = pl.program_id(0)
    at = 0
    for keep, send, (count, pieces, steps, fresh) in zip(outs[::2], outs[1::2], jobs):
        left, refs = refs[:count], refs[count:]
        right, refs = refs[:pieces], refs[pieces:]
        rows = sum(one.shape[0] for one in left)

        if fresh:

            @pl.when(step == at)
            def _():
                flip(flipped, left)

        @pl.when((step >= at) & (step < at + steps))
        def _():
            value = dot(flipped[:, :rows], jnp.concatenate([one[...] for one in right], axis=0))
            give_out(core[0], keep, send, slice(None), value)

        at += steps


def weight_grad(core, parts, jobs, after=()):
    width = jobs[0][0][0].shape[1]
    each = width // parts
    kinds, specs, given, outs, kept, at, most, last_left = [], [], [], [], [], 0, 0, None
    for left, right in jobs:
        wide = right[0].shape[1]
        block = math.gcd(wide, 1024)
        steps = wide // block
        most = max(most, sum(one.shape[0] for one in left))
        column = lambda j, at=at, last=steps - 1: jnp.clip(j - at, 0, last)
        specs += [whole(*one.shape) for one in left]
        specs += [
            pl.BlockSpec((one.shape[0], block), lambda j, column=column: (0, column(j)))
            for one in right
        ]
        given += [*left, *right]
        outs += [
            pl.BlockSpec((parts // 2, each, block), lambda j, column=column: (0, 0, column(j)))
        ] * 2
        kept += [shape((parts // 2, each, wide), BF)] * 2
        kinds.append((len(left), len(right), steps, left is not last_left))
        last_left = left
        at += steps
    return call(
        functools.partial(weight_grad_kernel, kinds),
        (at,),
        [SMEM] + specs,
        outs,
        kept,
        scratch=[pltpu.VMEM((width, most), BF)],
        flops=2 * most * width * sum(job[1][0].shape[1] for job in jobs),
        name="weight_grad",
        after=after,
    )(core, *given)


def head_grad_kernel(count, with_out, core, *refs):
    first, backs, refs = refs[:2], refs[2 : 2 + 2 * count], refs[2 + 2 * count :]
    keep, send, flipped = refs[-3:]
    flip(flipped, first)
    at = 0
    for i in range(count):
        right = jnp.concatenate([backs[2 * i][...], backs[2 * i + 1][...]], axis=0)
        wide = right.shape[1]
        give_out(core[0], keep, send, slice(at, at + wide), dot(flipped[...], right))
        at += wide
    if with_out:
        flip(flipped, refs[0:2])
        right = jnp.concatenate([refs[2][...], refs[3][...]], axis=0)
        give_out(core[0], keep, send, slice(at, at + right.shape[1]), dot(flipped[...], right))
    else:
        rows = [refs[0][...]]
        rows.append(jnp.zeros((PAIR - 4, rows[0].shape[1]), F32))
        value = jnp.concatenate(rows, axis=0).T
        give_out(core[0], keep, send, slice(at, at + PAIR), value)


def head_grad(core, parts, first, backs, out_job=(), terms=(), after=()):
    rows, width = first[0].shape
    each = width // parts
    total = sum(back[0].shape[1] for back in backs)
    total += out_job[2].shape[1] if out_job else PAIR
    given = [*first, *[half for pair in backs for half in pair], *out_job, *terms]
    out = whole(parts // 2, each, total)
    return call(
        functools.partial(head_grad_kernel, len(backs), bool(out_job)),
        (1,),
        [SMEM] + [whole(*one.shape) for one in given],
        [out] * 2,
        [shape((parts // 2, each, total), BF)] * 2,
        scratch=[pltpu.VMEM((width, 2 * rows), BF)],
        flops=4 * rows * width * total,
        name="head_grad",
        after=after,
    )(core, *given)


def res_back_kernel(
    species, own, other, cot, res0, res1, gain, w0, w1, *outs
):
    grad_out, attn_out, gm0_out, gm1_out, terms_out = outs
    res = jnp.where(pl.program_id(0) == 0, res0[...], res1[...])
    grad = own[...] + other[...].astype(F32)
    shaped, invert = normalize(res)
    made = cot[...].astype(F32) * species[0].astype(F32) + norm_back(
        grad, shaped, invert, gain[...]
    )
    grad_out[...] = made
    attn = made.astype(BF)
    attn_out[...] = attn
    gm1_out[...] = dot(attn, w1[...], NT).astype(BF)
    gm0_out[...] = dot(attn, w0[...], NT).astype(BF)

    @pl.when(pl.program_id(0) == 0)
    def _():
        terms_out[...] = jnp.zeros_like(terms_out)

    terms_out[0:1, :] += jnp.sum(grad * shaped, axis=0, keepdims=True)
    terms_out[1:2, :] += jnp.sum(grad, axis=0, keepdims=True)


def res_back(species, own, other, cot, res, gain, w0, w1, after=()):
    rows, width = own.shape
    mine = w0.shape[0]
    block = rows // 2
    row = lambda cols: pl.BlockSpec((block, cols), lambda i: (i, 0))
    return call(
        res_back_kernel,
        (rows // block,),
        [SMEM] + [row(width)] * 3 + [whole(block, width)] * 2
        + [whole(1, width)] + [whole(mine, width)] * 2,
        [row(width), row(width), row(mine), row(mine), whole(2, width)],
        [
            shape((rows, width), F32),
            shape((rows, width), BF),
            shape((rows, mine), BF),
            shape((rows, mine), BF),
            shape((2, width), F32),
        ],
        flops=4 * rows * width * mine,
        name="res_back",
        after=after,
    )(species, own, other, cot, *res, gain, w0, w1)


def first_back_kernel(count, half, *refs):
    sides, refs = (refs[: 3 * count], refs[3 * count : 6 * count]), refs[6 * count :]
    weights, tokens, (more, out1, out0, terms_out) = refs[:3], refs[3:5], refs[5:]

    @pl.when(pl.program_id(0) == 0)
    def _():
        terms_out[0:2, :] = jnp.zeros_like(more)
        terms_out[2:4, :] = more[...]

    for side, (backs, x, out) in enumerate(zip(sides, tokens, (out1, out0))):

        @pl.when(within(pl.program_id(0), side * half, half))
        def _():
            grad = None
            for i in range(3):
                beside = [one[...] for one in backs[i * count : (i + 1) * count]]
                term = dot(jnp.concatenate(beside, axis=1), weights[i][...], NT)
                grad = term if grad is None else grad + term
            out[...] = grad.astype(out.dtype)
            shaped, _ = normalize(x[...].astype(F32))
            terms_out[0:1, :] += jnp.sum(grad * shaped, axis=0, keepdims=True)
            terms_out[1:2, :] += jnp.sum(grad, axis=0, keepdims=True)


def first_back(groups, wq, wk, wv, tokens, terms, after=()):
    rows, width = tokens[0].shape
    mine = wq.shape[1]
    count = len(groups)
    block = math.gcd(rows, 256)
    half = rows // block
    given, specs = [], []
    for side in (1, 0):
        at = half * (1 - side)
        place = lambda i, at=at: (jnp.clip(i - at, 0, half - 1), 0)
        for kind in range(3):
            for group in groups:
                given.append(group[kind][side])
                specs.append(pl.BlockSpec((block, given[-1].shape[1]), place))
    outs = [
        pl.BlockSpec((block, width), lambda i, at=at: (jnp.clip(i - at, 0, half - 1), 0))
        for at in (0, half)
    ]
    return call(
        functools.partial(first_back_kernel, count, half),
        (2 * half,),
        specs + [whole(width, mine)] * 3 + outs + [whole(2, width)],
        outs + [whole(4, width)],
        [shape((rows, width), BF), shape((rows, width), F32), shape((4, width), F32)],
        flops=12 * rows * width * mine,
        name="first_back",
        after=after,
    )(*given, wq, wk, wv, tokens[1], tokens[0], terms)


def input_back_kernel(own, other, x, res, gain, out):
    shaped, invert = normalize(x[...].astype(F32))
    grad = own[...] + other[...].astype(F32)
    out[...] = res[...] + norm_back(grad, shaped, invert, gain[...])


def input_back(own, other, x, res, gain, after=()):
    rows, width = x.shape
    block = math.gcd(rows, 128)
    row = pl.BlockSpec((block, width), lambda i: (i, 0))
    return call(
        input_back_kernel,
        (rows // block,),
        [row] * 4 + [whole(1, width)],
        [row],
        [shape((rows, width), F32)],
        name="input_back",
        after=after,
    )(own, other, x, res, gain)[0]


def output_kernel(res0, res1, own, other, out):
    res = jnp.where(pl.program_id(0) == 0, res0[...], res1[...])
    out[...] = (res + own[...] + other[...].astype(F32)).astype(out.dtype)


def add_output(res, own, other, after=()):
    rows, width = own.shape
    block = rows // 2
    row = pl.BlockSpec((block, width), lambda i: (i, 0))
    return call(
        output_kernel,
        (2,),
        [whole(block, width)] * 2 + [row] * 2,
        [row],
        [shape((rows, width), BF)],
        name="add_output",
        after=after,
    )(*res, own, other)[0]


def pair_swap(values):
    return lax.ppermute(values, "tensor", [(0, 1), (1, 0)])


def dp_swap(values, turn, parts):
    return lax.ppermute(values, "dp", [(i, i ^ turn) for i in range(parts)])


def within(step, start, steps):
    return (step >= start) & (step < start + steps)


def total_of(refs):
    total = refs[0][...].astype(F32)
    for one in refs[1:]:
        total = total + one[...].astype(F32)
    return total


def combine_kernel(spans, places, *refs):
    count = sum(terms * shares for _, _, terms, shares in spans)
    ins, outs = refs[:count], refs[count:]
    for start, steps, terms, shares in spans:
        given, ins = ins[: terms * shares], ins[terms * shares :]
        made, outs = outs[:shares], outs[shares:]

        @pl.when(within(pl.program_id(0), start, steps))
        def _():
            for r in range(shares):
                made[r][...] = total_of(given[r * terms : (r + 1) * terms]).astype(BF)


class Scatter:
    def __init__(self, keep, send, order, count, place):
        self.count, self.place, self.order = count, place, list(order)
        self.left = list(range(count.bit_length() - 2, 0, -1))
        self.parts = [keep, dp_swap(send, 1, count)]


def advance(chains, after=()):
    chains = [chain for chain in chains if chain.order]
    if not chains:
        return tuple(after)
    spans, places, given, ins, outs, shapes, begin = [], [], [], [], [], [], 0
    for i, chain in enumerate(chains):
        bits = chain.order.pop(0)
        shares = 2 ** len(bits)
        axis = chain.left.index(bits[-1])
        for bit in bits:
            chain.left.remove(bit)
        each, columns = chain.parts[0].shape[-2:]
        high, low = 2**axis, 2 ** (len(chain.left) - axis)
        view = (high, shares, low, each, columns)
        block = 1024 if columns % 1024 == 0 else columns
        last = columns // block - 1
        block_of = lambda j, begin=begin, last=last: jnp.clip(j - begin, 0, last)
        for r in range(shares):
            share = pl.BlockSpec(
                (high, None, low, each, block),
                lambda j, at, i=i, r=r, block_of=block_of: (0, at[i] ^ r, 0, 0, block_of(j)),
            )
            ins += [share] * len(chain.parts)
            given += [one.reshape(view) for one in chain.parts]
        out = pl.BlockSpec(
            (high, low, each, block), lambda j, at, block_of=block_of: (0, 0, 0, block_of(j))
        )
        outs += [out] * shares
        shapes += [shape((high, low, each, columns), BF)] * shares
        spans.append((begin, last + 1, len(chain.parts), shares))
        places.append((chain.place >> bits[0]) & (shares - 1))
        chain.bits, chain.shares = bits, shares
        begin += last + 1
    made = call(
        functools.partial(combine_kernel, spans),
        (begin,),
        ins,
        outs,
        shapes,
        name="combine",
        after=after,
        scalars=1,
    )(jnp.stack(places).astype(jnp.int32), *given)
    first = made[0]
    for chain in chains:
        own, made = made[: chain.shares], made[chain.shares :]
        chain.parts = [own[0]] + [
            dp_swap(own[r], r << chain.bits[0], chain.count) for r in range(1, chain.shares)
        ]
    return (first,)


def finish_kernel(counts, cuts, *refs):
    total = sum(counts)
    ins, outs = refs[:total], refs[total:]
    for count, cut in zip(counts, cuts):
        given, ins = ins[:count], ins[count:]
        value = total_of(given)
        for at, wide, to in cut:
            out, low = outs[to[0]], to[1]
            out[:, low : low + wide] = value[:, at : at + wide]


def finish(chains, cuts, columns, after=()):
    while any(chain.order for chain in chains):
        after = advance(chains, after)
    given, counts = [], []
    for chain in chains:
        flat = chain.parts[0].shape[-2:]
        counts.append(len(chain.parts))
        given += [one.reshape(flat) for one in chain.parts]
    rows = given[0].shape[0]
    return call(
        functools.partial(finish_kernel, counts, cuts),
        (1,),
        [whole(*one.shape) for one in given],
        [whole(rows, wide) for wide in columns],
        [shape((rows, wide), F32) for wide in columns],
        name="finish",
        after=after,
    )(*given)


def body(
    parts,
    tokens,
    cotangent,
    species,
    wq,
    wk,
    wv,
    wo,
    first_gain,
    first_bias,
    second_gain,
    second_bias,
    wg,
    wu,
    wd,
):
    place = lax.axis_index("dp")
    half = lax.axis_index("tensor")
    core = (place & 1).astype(jnp.int32).reshape(1)
    rows = tokens.shape[0]
    bits = parts.bit_length() - 1
    wide = [[bit] for bit in range(2, bits)]
    low_first = [[1]] * (bits > 1) + wide
    high_first = wide + [[1]] * (bits > 1)
    first_gain, first_bias = first_gain[None], first_bias[None]
    second_gain, second_bias = second_gain[None], second_bias[None]

    tokens1 = pair_swap(tokens)
    cot1 = pair_swap(cotangent)
    table0 = rotary_tables(half * rows, rows)
    table1 = rotary_tables((1 - half) * rows, rows)
    first0, q0, k0, v0 = project(tokens, first_gain, first_bias, wq, wk, wv, table0)
    gr0, grad_hidden0 = scale_rows(species, cotangent, wd, after=(first0,))
    first1, q1, k1, v1 = project(
        tokens1, first_gain, first_bias, wq, wk, wv, table1, after=(gr0,)
    )
    mixed1, lse1 = attend(q1, k0, k1, v0, v1)
    cut = rows // 2
    attn_a = product_part(0, cut, mixed1, wo)
    attn_b = product_part(cut, rows - cut, mixed1, wo, after=(attn_a,))
    got_a, got_b = pair_swap(attn_a), pair_swap(attn_b)
    mixed0, lse0 = attend(q0, k0, k1, v0, v1, after=(attn_b,))
    gr1, grad_hidden1 = scale_rows(species, cot1, wd, after=(mixed0,))
    second = lambda start, got, more, after: residual(
        start, cut, tokens, mixed0, wo, got, second_gain, second_bias, more, after=after
    )
    res_a, second0a = second(0, got_a, 0, (grad_hidden1,))
    res_b, second0b, wo_late = second(cut, got_b, 1, (res_a,))
    res = (res_a, res_b)
    second1a, second1b = pair_swap(second0a), pair_swap(second0b)
    wo1 = pair_swap(wo_late)
    hid0, gb0, ub0, st0, ff0 = feed((second0a, second0b), grad_hidden0, wg, wu, F32, wd)
    hid1, gb1, ub1, st1 = feed((second1a, second1b), grad_hidden1, wg, wu, BF, after=mark((st0, second1a)))

    st_got = pair_swap(st1)
    seconds = [second0a, second0b, second1a, second1b]
    gate_keep, gate_send, up_keep, up_send = weight_grad(
        core, parts, [(seconds, [gb0, gb1]), (seconds, [ub0, ub1])], after=(st1,)
    )
    gate = Scatter(gate_keep, gate_send, low_first, parts, place)
    up = Scatter(up_keep, up_send, high_first, parts, place)
    down_keep, down_send = weight_grad(
        core, parts, [([gr0, gr1], [hid0, hid1])], after=(gate_keep, wo1)
    )
    down = Scatter(down_keep, down_send, low_first, parts, place)
    grad_res, attn_grad0, gm0, gm_give, second_terms = res_back(
        species, st0, st_got, cotangent, res, second_gain, wo, wo1, after=(down_keep,)
    )
    gm1 = pair_swap(gm_give)
    attn_grad1 = pair_swap(attn_grad0)
    step = advance([gate], after=(grad_res,))
    step = advance([up], after=step)
    step = advance([down], after=step)

    pairs = q0.shape[1] // PAIR
    back = lambda start, stop, after: attend_back(
        start,
        stop,
        (q0, q1),
        (k0, k1),
        (v0, v1),
        (gm0, gm1),
        (mixed0, mixed1),
        (lse0, lse1),
        (table0[0], table1[0]),
        (table0[1], table1[1]),
        after=after,
    )
    cut = pairs // 2
    firsts = (first0, first1)
    low = back(0, cut, step)
    ff1 = down_product(hid1, wd, after=(low[0][0],))
    ff_got = pair_swap(ff1)
    step = advance([gate], after=(ff1,))
    step = advance([up], after=step)
    low_keep, low_send = head_grad(
        core, parts, firsts, low, out_job=(attn_grad0, attn_grad1, mixed0, mixed1), after=step
    )
    heads0 = Scatter(low_keep, low_send, low_first, parts, place)
    high = back(cut, pairs, (low_keep,))
    step = advance([down], after=(high[0][0],))
    step = advance([gate], after=step)
    step = advance([up], after=step)
    step = advance([heads0], after=step)
    ft1, ft0, terms = first_back(
        (low, high), wq, wk, wv, (tokens, tokens1), second_terms, after=step
    )
    ft_got = pair_swap(ft1)
    high_keep, high_send = head_grad(core, parts, firsts, high, terms=(terms,), after=(ft1,))
    heads1 = Scatter(high_keep, high_send, low_first, parts, place)
    output = add_output(res, ff0, ff_got, after=(high_keep,))
    step = advance([down], after=mark((output, *gate.parts, *up.parts)))
    step = advance([heads0], after=step)
    step = advance([heads1], after=step)
    step = advance([heads0], after=mark((*step, *down.parts)))
    step = advance([heads1], after=step)
    step = advance([heads1], after=step)
    input_grad = input_back(ft0, ft_got, tokens, grad_res, first_gain, after=step)
    step = (input_grad,)
    hidden = wg.shape[1]
    mine = wq.shape[1]
    one, two = cut * PAIR, mine - cut * PAIR
    all_of = lambda to: [(0, hidden, (to, 0))]
    query_sum, key_sum, value_sum, out_sum, norm_sum = finish(
        [heads0, heads1],
        [
            [(i * one, one, (i, 0)) for i in range(3)] + [(3 * one, mine, (3, 0))],
            [(i * two, two, (i, one)) for i in range(3)] + [(3 * two, PAIR, (4, 0))],
        ],
        [mine] * 4 + [PAIR],
        after=step,
    )
    gate_sum, up_sum, down_sum = finish(
        [gate, up, down], [all_of(i) for i in range(3)], [hidden] * 3, after=(query_sum,)
    )
    norm_sum = norm_sum[:, :4]
    norm_sum = norm_sum + pair_swap(norm_sum)
    return (
        output,
        input_grad,
        query_sum,
        key_sum,
        value_sum,
        out_sum.T,
        gate_sum,
        up_sum,
        down_sum.T,
        norm_sum.T,
    )


def solution(mesh):
    in_specs = (
        P(("dp", "tensor"), None),
        P(("dp", "tensor"), None),
        P("dp"),
        P(None, "tensor"),
        P(None, "tensor"),
        P(None, "tensor"),
        P("tensor", None),
        P(),
        P(),
        P(),
        P(),
        P(None, "tensor"),
        P(None, "tensor"),
        P("tensor", None),
    )
    out_specs = (
        P(("dp", "tensor"), None),
        P(("dp", "tensor"), None),
        P("dp", "tensor"),
        P("dp", "tensor"),
        P("dp", "tensor"),
        P("tensor", "dp"),
        P("dp", "tensor"),
        P("dp", "tensor"),
        P("tensor", "dp"),
        P(None, "dp"),
    )
    return jax.shard_map(
        functools.partial(body, mesh.shape["dp"]),
        mesh=mesh,
        in_specs=in_specs,
        out_specs=out_specs,
        check_vma=False,
    )
```
